256 devices in a mesh: inst: 16 (over x, y_hi, core), tp: 16 (over z, y_lo).
Axes of the slice: x: 4, y: 4 (y_hi: 2, y_lo: 2; y = y_hi * 2 + y_lo), z: 8, core: 2. Of those that a mesh axis runs over, the one named last changes fastest.
Arguments:
- fresh_segment_probes: bfloat16 [4096, 64, 128], P('inst', 'tp'), may hold values from -10 to 10
- fresh_segment_pairs: bfloat16 [4096, 2, 16, 128], P('inst', None, 'tp'), may hold values from -5 to 5
- earlier_stored_pairs: bfloat16 [16384, 2, 16, 128], P('inst', None, 'tp'), may hold values from -5 to 5
- emitted_token_probe: bfloat16 [64, 128], P('tp'), may hold values from -10 to 10
- emitted_token_pair: bfloat16 [2, 16, 128], P(None, 'tp'), may hold values from -5 to 5
- final_projection_weights: bfloat16 [8192, 8192], P('tp', 'inst'), may hold values from -0.0625 to 0.0625
- remaining_instance_ids: int32 [8], replicated, may hold values from 0 to 15, as said below
- segment_destination_member: int32 [32, 1], replicated, may hold values from 0 to 7; in each aligned block of 32 rows (0 to 31, 32 to 63, ...) at most 8 rows name the same one
Outputs:
- span_hidden: bfloat16 [4096, 8192], P('inst', 'tp')
- migrated_cache: bfloat16 [16, 1024, 2, 16, 128], P('inst', None, None, 'tp')
- decode_attention: bfloat16 [64, 128], P('tp')
The draws below stay inside these ranges and needn't reach their ends.
Inputs may be any that keep to these rules, and one draw needn't show every extreme that they name: `segment_destination_member`: at most 8 blocks name one survivor, a bound that some block reaches. `remaining_instance_ids`: 8 distinct instance indices; instances 0 and 15 always survive.
All inputs are finite; a program needn't handle non-finite values.
Results may differ from the reference program's by a relative error of at most 0.024.
Values may be sent and summed in bfloat16 or wider, within the bound.
A program may use at most 128 MiB of HBM per device.

```python
import math
import jax
import jax.numpy as jnp
import numpy as np
from jax import lax

D = 8192
HQ = 64
KVH = 8
HD = 128
BLK = 128
INSTANCES = 16
KVS = 16
SURV = 8
SPAN = 4096
PREFIX = 16384
NBLK = 32
CAP = 8
N_TP = 16


def drawn_parts(key):
    first = jax.random.randint(jax.random.fold_in(key, 102), (KVH,), 0, PREFIX)
    offset = jax.random.randint(jax.random.fold_in(key, 103), (KVH,), 1, PREFIX)
    second = (first + offset) % PREFIX
    chosen_rows = jax.random.randint(jax.random.fold_in(key, 104), (4,), 0, SPAN)
    return (first, second, chosen_rows)


def shared_direction(key):
    return jnp.clip(jax.random.normal(jax.random.fold_in(key, 201), (KVH, HD), jnp.float32), -3.0, 3.0)


def spread_slots(array, reduce_dimension):
    return jnp.repeat(array, KVS // KVH, axis=reduce_dimension)


def draw_earlier_stored_pairs(key, part):
    first, second, chosen_rows = drawn_parts(key)
    key = jax.random.fold_in(key, 1)
    base = jnp.clip(jax.random.normal(key, (PREFIX, 2, KVH, HD), jnp.float32), -5.0, 5.0)
    strength = 0.0
    positions = jnp.arange(PREFIX)[:, None]
    hit_first = (positions == first[None, :]).astype(jnp.float32)
    hit_second = (positions == second[None, :]).astype(jnp.float32)
    weight = jnp.minimum(hit_first + hit_second, 1.0)[..., None] * strength
    keys = base[:, 0] * (1.0 - weight)
    full = jnp.stack([keys, 0.5 * base[:, 1]], axis=1)
    return spread_slots(full, 2).astype(jnp.bfloat16)


def draw_fresh_segment_probes(key, part):
    first, second, chosen_rows = drawn_parts(key)
    key = jax.random.fold_in(key, 2)
    base = jnp.clip(2.5 * jax.random.normal(key, (SPAN, HQ, HD), jnp.float32), -10.0, 10.0)
    strength = 0.0
    hits = (jnp.arange(SPAN)[:, None] == chosen_rows[None, :]).astype(jnp.float32)
    weight = jnp.minimum(jnp.sum(hits, axis=1), 1.0)[:, None, None] * strength
    return (base * (1.0 - weight)).astype(jnp.bfloat16)


def draw_emitted_token_probe(key, part):
    common = shared_direction(key)
    key = jax.random.fold_in(key, 3)
    base = 2.5 * jax.random.normal(key, (HQ, HD), jnp.float32)
    strength = 0.0
    head_index = jnp.arange(HQ) * KVH // HQ
    base = jnp.clip(base + common[head_index], -10.0, 10.0)
    picks = jax.random.bernoulli(jax.random.fold_in(key, 31), 0.5, (HQ,)).astype(jnp.float32)
    weight = picks[:, None] * strength
    return (base * (1.0 - weight)).astype(jnp.bfloat16)


def draw_fresh_segment_pairs(key, part):
    key = jax.random.fold_in(key, 4)
    base = jnp.clip(jax.random.normal(key, (SPAN, 2, KVH, HD), jnp.float32), -5.0, 5.0)
    full = jnp.stack([base[:, 0], 0.5 * base[:, 1]], axis=1)
    return spread_slots(full, 2).astype(jnp.bfloat16)


def draw_emitted_token_pair(key, part):
    common = shared_direction(key)
    key = jax.random.fold_in(key, 5)
    values = jnp.clip(jax.random.normal(key, (KVH, HD), jnp.float32), -5.0, 5.0)
    base = jnp.stack([common, 0.5 * values], axis=0)
    return spread_slots(base, 1).astype(jnp.bfloat16)


def draw_remaining_instance_ids(key, part):
    key = jax.random.fold_in(key, 6)
    middle = jax.random.permutation(key, INSTANCES - 2)[:SURV - 2].astype(jnp.int32) + 1
    chosen = jnp.concatenate([jnp.array([0, INSTANCES - 1], jnp.int32), middle])
    order = jax.random.permutation(jax.random.fold_in(key, 61), SURV)
    return chosen[order].astype(jnp.int32)


def block_scale(key, dims, shards, least, top_value):
    def one(axis_at, shards_of):
        steps = jax.random.uniform(jax.random.fold_in(jax.random.fold_in(key, 6), axis_at), (shards_of,), jnp.float32, least / len(shards), top_value / len(shards))
        return jnp.repeat(jnp.exp(steps), dims[axis_at] // shards_of).reshape((-1,) + (1,) * (len(dims) - axis_at - 1))

    level = one(*shards[0])
    for cut in shards[1:]:
        level = level * one(*cut)
    return level


def routed_block(key, own, number, rows, number_of, top, bound, skew):
    order = jax.random.permutation(key, number_of)
    crowded, usual = load_shares(number_of, rows * top, bound, skew, True), load_shares(number_of, rows * top, bound, skew, False)
    places = jnp.arange(number_of)

    def named(tallies, offset_by):
        used = int((tallies > 0).sum())
        fixed = max(1, used // 4)
        passed = fixed + (places - fixed + offset_by * (used - fixed)) % max(1, number_of - fixed)
        return jnp.zeros((number_of,), jnp.int32).at[order[jnp.where(places < fixed, places, passed)]].set(jnp.asarray(tallies, jnp.int32))

    tallies = jnp.where(number % 4 == 0, named(crowded, number // 4), named(usual, number - number // 4 - 1))
    mixed = jax.random.permutation(jax.random.fold_in(own, 3), number_of)
    source_of, sink = mixed[0:number_of // 2 * 2:2], mixed[1:number_of // 2 * 2:2]
    margin = jnp.minimum(tallies[source_of] - 1, bound - tallies[sink]) // 2
    margin = jnp.where((source_of == order[0]) | (sink == order[0]) | (tallies[sink] == 0), 0, jnp.maximum(margin, 0))
    passed = jax.random.randint(jax.random.fold_in(own, 4), (number_of // 2,), 0, 1 << 20) % (margin + 1)
    tallies = tallies.at[source_of].add(-passed).at[sink].add(passed)
    members = jnp.searchsorted(jnp.cumsum(tallies), jnp.arange(rows * top), side="right").astype(jnp.int32)
    table = members.reshape(top, rows).T
    table = table[jax.random.permutation(jax.random.fold_in(own, 1), rows)]
    offset_by = jax.random.randint(jax.random.fold_in(own, 2), (rows, 1), 0, top)
    return jnp.take_along_axis(table, (jnp.arange(top)[None, :] + offset_by) % top, axis=1)


def load_shares(amount, total, bound, skew, full):
    weights = [(1 << 20) // math.isqrt(rank ** skew) + 1 for rank in range(1, amount + 1)]
    largest = bound if full else min(bound, max(-(-total // amount), total * weights[0] // sum(weights)))
    least = 1 if total - largest >= amount - 1 else 0
    counts, surplus = [largest] + [least] * (amount - 1), total - largest - least * (amount - 1)
    while surplus > 0:
        movable = [i for i in range(1, amount) if counts[i] < largest] or [i for i in range(1, amount) if counts[i] < bound]
        mass, budget = sum([weights[i] for i in movable]), surplus
        for i in movable:
            addition = min(bound - counts[i], max(1, budget * weights[i] // mass), surplus)
            counts[i] = counts[i] + addition
            surplus = surplus - addition
    return np.array(counts)


def scatter_about(own_key, shape, scale, bound, split=(), held_as=jnp.bfloat16):
    factor_of = block_scale(own_key, shape, split, -0.22, 0.18) if split else 1.0
    entries = jax.random.normal(own_key, shape, jnp.float32) * scale * factor_of
    return jnp.minimum(jnp.maximum(entries, -bound), bound).astype(held_as)


def setup_inputs(seed: int = 0) -> dict:
    splits = jax.random.split(jax.random.key(seed), 9)
    fresh_segment_probes = draw_fresh_segment_probes(jax.random.fold_in(splits[8], 71), 0)
    fresh_segment_pairs = draw_fresh_segment_pairs(jax.random.fold_in(splits[8], 71), 0)
    earlier_stored_pairs = draw_earlier_stored_pairs(jax.random.fold_in(splits[8], 71), 0)
    emitted_token_probe = draw_emitted_token_probe(jax.random.fold_in(splits[8], 71), 0)
    emitted_token_pair = draw_emitted_token_pair(jax.random.fold_in(splits[8], 71), 0)
    final_projection_weights = scatter_about(splits[5], (HQ * HD, D), (HQ * HD) ** -0.5, 0.0625, ((0, 16), (1, 16)))
    remaining_instance_ids = draw_remaining_instance_ids(jax.random.fold_in(splits[8], 71), 0)
    segment_destination_member_keys = jax.random.split(jax.random.fold_in(splits[7], 1), NBLK // NBLK)
    segment_destination_member_turns = jax.random.permutation(jax.random.fold_in(splits[7], 3), NBLK // NBLK)
    segment_destination_member = jax.vmap(lambda own, number: routed_block(jax.random.fold_in(splits[7], 2), own, number, NBLK, SURV, 1, CAP, 2))(segment_destination_member_keys, segment_destination_member_turns).reshape((NBLK, 1))
    return dict(fresh_segment_probes=fresh_segment_probes, fresh_segment_pairs=fresh_segment_pairs, earlier_stored_pairs=earlier_stored_pairs, emitted_token_probe=emitted_token_probe, emitted_token_pair=emitted_token_pair, final_projection_weights=final_projection_weights, remaining_instance_ids=remaining_instance_ids, segment_destination_member=segment_destination_member)


def rounded_weights(scores):
    highest = jnp.max(scores, axis=-1, keepdims=True)
    weights = jnp.exp(scores - highest)
    total = jnp.sum(weights, axis=-1)
    kept = lax.optimization_barrier(weights.astype(jnp.bfloat16)).astype(jnp.float32)
    return kept, total


def reference(fresh_segment_probes, fresh_segment_pairs, earlier_stored_pairs, emitted_token_probe, emitted_token_pair, final_projection_weights, remaining_instance_ids, segment_destination_member):
    scale = HD ** -0.5
    group = HQ // KVS
    keys_all = jnp.concatenate([earlier_stored_pairs, fresh_segment_pairs], axis=0)
    queries = fresh_segment_probes.reshape(SPAN, KVS, group, HD)
    rows_block = math.gcd(512, SPAN)
    block_count = SPAN // rows_block
    zero = jnp.zeros((), jnp.int32)
    key_positions = jnp.arange(PREFIX + SPAN, dtype=jnp.int32)

    def one_block(index):
        row_block = (index // KVS).astype(jnp.int32)
        slot = (index % KVS).astype(jnp.int32)
        start = (row_block * rows_block).astype(jnp.int32)
        query = lax.dynamic_slice(queries, (start, slot, zero, zero), (rows_block, 1, group, HD))[:, 0].astype(jnp.float32)
        pairs = lax.dynamic_index_in_dim(keys_all, slot, axis=2, keepdims=False)
        keys = pairs[:, 0].astype(jnp.float32)
        values = pairs[:, 1].astype(jnp.float32)
        scores = jnp.einsum("rgd,nd->rgn", query, keys) * scale
        row_positions = PREFIX + start + jnp.arange(rows_block, dtype=jnp.int32)
        visible = key_positions[None, :] <= row_positions[:, None]
        scores = jnp.where(visible[:, None, :], scores, -jnp.inf)
        kept, total = rounded_weights(scores)
        summed = jnp.einsum("rgn,nd->rgd", kept, values)
        return (summed / total[..., None]).astype(jnp.bfloat16)

    blocks = lax.map(one_block, jnp.arange(block_count * KVS, dtype=jnp.int32))
    blocks = blocks.reshape(block_count, KVS, rows_block, group, HD)
    attention = jnp.transpose(blocks, (0, 2, 1, 3, 4)).reshape(SPAN, HQ * HD)

    group_width = HQ * HD // N_TP

    def add_group(total, index):
        left = lax.dynamic_slice_in_dim(attention, (index * group_width).astype(jnp.int32), group_width, 1)
        right = lax.dynamic_slice_in_dim(final_projection_weights, (index * group_width).astype(jnp.int32), group_width, 0)
        part = jnp.dot(left, right, preferred_element_type=jnp.float32)
        part = lax.optimization_barrier(part.astype(jnp.bfloat16)).astype(jnp.float32)
        return total + part, None

    hidden_sum, unused = lax.scan(add_group, jnp.zeros((SPAN, D), jnp.float32), jnp.arange(N_TP, dtype=jnp.int32))
    span_hidden = hidden_sum.astype(jnp.bfloat16)

    destination_sequence = segment_destination_member[:, 0]
    destination_agreement = (destination_sequence[:, None] == jnp.arange(SURV, dtype=jnp.int32)[None, :]).astype(jnp.int32)
    slots = (jnp.sum(jnp.cumsum(destination_agreement, axis=0) * destination_agreement, axis=1) - 1).astype(jnp.int32)
    destination_members = remaining_instance_ids[destination_sequence].astype(jnp.int32)
    pieces = fresh_segment_pairs.reshape(NBLK, BLK, 2, KVS, HD)
    cache = jnp.zeros((INSTANCES, CAP, BLK, 2, KVS, HD), jnp.bfloat16).at[destination_members, slots].set(pieces)
    migrated_cache = cache.reshape(INSTANCES, CAP * BLK, 2, KVS, HD)

    every_key = jnp.concatenate([keys_all, emitted_token_pair[None]], axis=0).astype(jnp.float32)
    single = emitted_token_probe.reshape(KVS, group, HD).astype(jnp.float32)
    decode_scores = jnp.einsum("sgd,nsd->sgn", single, every_key[:, 0]) * scale
    kept, total = rounded_weights(decode_scores)
    summed = jnp.einsum("sgn,nsd->sgd", kept, every_key[:, 1])
    decode_attention = (summed / total[..., None]).astype(jnp.bfloat16).reshape(HQ, HD)
    return span_hidden, migrated_cache, decode_attention
```

```python
import functools
import jax
import jax.numpy as jnp
from jax import lax
from jax.experimental import pallas as pl
from jax.experimental.pallas import tpu as pltpu
from jax.sharding import PartitionSpec as P

BLK = 128
CAP = 8
ROWS = 256
HEADS = 4
HD = 128
Q = ROWS * HEADS
KEYS = 1280
PIECE = 256
NX = 4
NS = 4
NZ = 8
NEG = -1e30
C2 = float(HD ** -0.5 * 1.4426950408889634)
MESH = pl.DeviceIdType.MESH


def signal(where):
    pl.semaphore_signal(
        pltpu.get_barrier_semaphore(), inc=1, device_id=where, device_id_type=MESH
    )


def attention_kernel(
    q_hbm, k_hbm, vt_hbm, probe_ref, pair_ref,
    a_ref, dec_ref,
    qbuf, kbuf, vbuf, acc, m_s, l_s, s_buf,
    o_send, o_recv, st_send, st_recv, qd, d_all,
    loc_sem, q_ss, q_rs, k_ss, k_rs, v_ss, v_rs, o_ss, o_rs, t_ss, t_rs, d_ss, d_rs,
):
    me = lax.axis_index("inst")
    x, s = me // NS, me % NS
    s1 = s + 1 - 2 * (s % 2)
    s2 = (s + 2) % NS
    s3 = (s1 + 2) % NS

    def at_x(d):
        return {"inst": ((x + d) % NX) * NS + s}

    def at_s(t):
        return {"inst": x * NS + t}

    def remote(src, dst, ss, rs, where):
        return pltpu.make_async_remote_copy(
            src_ref=src, dst_ref=dst, send_sem=ss, recv_sem=rs,
            device_id=where, device_id_type=MESH,
        )

    own = [
        pltpu.make_async_copy(k_hbm, kbuf.at[s], loc_sem.at[0]),
        pltpu.make_async_copy(q_hbm, qbuf.at[0], loc_sem.at[1]),
        pltpu.make_async_copy(vt_hbm, vbuf.at[s], loc_sem.at[2]),
    ]
    for copy in own:
        copy.start()

    for d in (1, 2, 3):
        signal(at_x(d))
    signal(at_s(s1))
    signal(at_s(s2))
    pl.semaphore_wait(pltpu.get_barrier_semaphore(), 5)

    def q_push(d):
        return remote(q_hbm, qbuf.at[NX - d], q_ss.at[d - 1], q_rs.at[NX - d - 1], at_x(d))

    k_push = [
        remote(k_hbm, kbuf.at[s], k_ss.at[0], k_rs.at[0], at_s(s1)),
        remote(k_hbm, kbuf.at[s], k_ss.at[1], k_rs.at[1], at_s(s2)),
        remote(kbuf.at[s2], kbuf.at[s2], k_ss.at[2], k_rs.at[2], at_s(s1)),
    ]
    v_push = [
        remote(vt_hbm, vbuf.at[s], v_ss.at[0], v_rs.at[0], at_s(s1)),
        remote(vt_hbm, vbuf.at[s], v_ss.at[1], v_rs.at[1], at_s(s2)),
        remote(vbuf.at[s2], vbuf.at[s2], v_ss.at[2], v_rs.at[2], at_s(s1)),
    ]
    k_push[0].start()
    q_push(1).start()
    q_push(3).start()
    v_push[0].start()
    k_push[1].start()
    v_push[1].start()

    qd[...] = jnp.zeros_like(qd)
    qd[0:HEADS, :] = probe_ref[...]
    acc[...] = jnp.zeros_like(acc)
    l_s[...] = jnp.zeros_like(l_s)
    m_s[...] = jnp.full(m_s.shape, NEG, jnp.float32)

    key_of = lax.broadcasted_iota(jnp.int32, (PIECE, Q), 0)
    row_of = lax.broadcasted_iota(jnp.int32, (PIECE, Q), 1) % ROWS

    def scores(buf, q, k, j, highest):
        part = lax.dot_general(
            kbuf[k, j * PIECE:(j + 1) * PIECE, :], qbuf[q],
            (((1,), (1,)), ((), ())), preferred_element_type=jnp.float32,
        )
        if j == KEYS // PIECE - 1:
            ahead = ROWS * (((x + q) % NX) * NS + s - (x * NS + k))
            part = jnp.where(key_of - row_of <= ahead, part, NEG)
        s_buf[buf, j * PIECE:(j + 1) * PIECE, :] = part
        return jnp.maximum(highest, jnp.max(part.reshape(PIECE // 8, 8, Q), axis=0))

    lowest = jnp.full((8, Q), NEG, jnp.float32)

    def unit(buf, q, k, highest, following):
        m_old = m_s[q]
        m_new = jnp.maximum(
            m_old, jnp.broadcast_to(jnp.max(highest, axis=0, keepdims=True), (8, Q))
        )
        m_s[q] = m_new
        alpha = jnp.exp2((m_old - m_new) * C2)
        top = m_new[0:1]
        total = acc[q] * alpha[0:1]
        norm = l_s[q] * alpha
        after = lowest
        for j in range(KEYS // PIECE):
            if following is not None:
                after = scores(1 - buf, following[0], following[1], j, after)
            p = jnp.exp2((s_buf[buf, j * PIECE:(j + 1) * PIECE, :] - top) * C2)
            norm = norm + jnp.sum(p.reshape(PIECE // 8, 8, Q), axis=0)
            total = total + jnp.dot(
                vbuf[k, :, j * PIECE:(j + 1) * PIECE], p.astype(jnp.bfloat16),
                preferred_element_type=jnp.float32,
            )
        acc[q] = total
        l_s[q] = norm
        return after

    def q_at(i):
        phase, n = i // 4, i % 4
        near = n + n // 2 - 2 * (n // 3)
        far = 2 - n + 3 * (n // 2) - 2 * (n // 3)
        return near * (1 - phase) + far * phase

    def k_at(i):
        phase = i // 4
        return s * (1 - phase) + s2 * phase, s1 * (1 - phase) + s3 * phase

    def normalised(q, t):
        cols = slice(t * 128, (t + 1) * 128)
        norm = jnp.sum(l_s[q, :, cols], axis=0, keepdims=True)
        return acc[q, :, cols] / norm, m_s[q, 0:1, cols] * C2 + jnp.log2(norm)

    def o_push(d):
        return remote(
            o_send.at[d - 1], o_recv.at[NX - d - 1], o_ss.at[d - 1], o_rs.at[NX - d - 1], at_x(d)
        )

    def t_push(d):
        return remote(
            st_send.at[d - 1], st_recv.at[NX - d - 1], t_ss.at[d - 1], t_rs.at[NX - d - 1], at_x(d)
        )

    for copy in own:
        copy.wait()
    highest = lowest
    for j in range(KEYS // PIECE):
        highest = scores(0, 0, s, j, highest)

    def pair(i, highest):
        q = q_at(i)
        ka, kb = k_at(i)

        @pl.when(i == 0)
        def _():
            k_push[0].wait_recv()
            v_push[0].wait_recv()

        @pl.when(i == 4)
        def _():
            k_push[2].wait_recv()
            v_push[2].wait_recv()

        highest = unit(0, q, ka, highest, (q, kb))

        @pl.when(i == 0)
        def _():
            q_push(1).wait_send()
            q_push(2).start()
            q_push(3).wait_recv()

        @pl.when(i == 1)
        def _():
            q_push(1).wait_recv()

        @pl.when(i == 2)
        def _():
            q_push(2).wait_recv()

        @pl.when(i == 3)
        def _():
            k_push[1].wait_recv()
            k_push[2].start()
            v_push[1].wait_recv()
            v_push[2].start()

        highest = unit(1, q, kb, highest, (q_at(i + 1), k_at(i + 1)[0]))

        @pl.when(i >= 4)
        def _():
            for t in range(Q // 128):
                o, lse = normalised(q, t)
                o_send[q - 1, :, t * 128:(t + 1) * 128] = o.astype(jnp.bfloat16)
                st_send[q - 1, t:t + 1, :] = lse
            o_push(q).start()
            t_push(q).start()

        return highest

    highest = lax.fori_loop(0, 7, pair, highest)
    highest = unit(0, 0, s2, highest, (0, s3))
    unit(1, 0, s3, highest, None)

    dm = jnp.full((1, 128), NEG, jnp.float32)
    dl = jnp.zeros((1, 128), jnp.float32)
    da = jnp.zeros((HD, 128), jnp.float32)
    for k in range(NS):
        part = lax.dot_general(
            kbuf[k], qd[...], (((1,), (1,)), ((), ())), preferred_element_type=jnp.float32
        )
        new = jnp.maximum(dm, jnp.max(part, axis=0, keepdims=True))
        alpha = jnp.exp2((dm - new) * C2)
        p = jnp.exp2((part - new) * C2)
        dl = dl * alpha + jnp.sum(p, axis=0, keepdims=True)
        da = da * alpha + jnp.dot(
            vbuf[k], p.astype(jnp.bfloat16), preferred_element_type=jnp.float32
        )
        dm = new
    d_all[x, 0:8, :] = jnp.transpose(da)[0:8]
    d_all[x, 8:16, :] = jnp.transpose(jnp.broadcast_to(dm, (128, 128)))[0:8]
    d_all[x, 16:24, :] = jnp.transpose(jnp.broadcast_to(dl, (128, 128)))[0:8]

    def d_push(d):
        return remote(d_all.at[x], d_all.at[x], d_ss.at[d - 1], d_rs.at[NX - d - 1], at_x(d))

    for d in (1, 2, 3):
        d_push(d).start()

    for d in (1, 2, 3):
        o_push(d).wait_recv()
        t_push(d).wait_recv()
    for t in range(Q // 128):
        cols = slice(t * 128, (t + 1) * 128)
        o, lse = normalised(0, t)
        rest = [st_recv[d, t:t + 1, :] for d in range(3)]
        top = functools.reduce(jnp.maximum, rest, lse)
        weight = jnp.exp2(lse - top)
        total, norm = o * weight, weight
        for d in range(3):
            weight = jnp.exp2(rest[d] - top)
            total = total + o_recv[d, :, cols].astype(jnp.float32) * weight
            norm = norm + weight
        h, r = t // 2, (t % 2) * 128
        a_ref[r:r + 128, h * HD:(h + 1) * HD] = jnp.transpose(total / norm).astype(jnp.bfloat16)

    for d in (1, 2, 3):
        d_push(d).wait_recv()
    query = qd[0:8, :].astype(jnp.float32)
    last = jnp.sum(query * pair_ref[0:1, :].astype(jnp.float32), axis=1, keepdims=True)
    last = jnp.broadcast_to(last, (8, HD))
    top = last
    for d in range(NX):
        top = jnp.maximum(top, d_all[d, 8:16, :])
    weight = jnp.exp2((last - top) * C2)
    total, norm = weight * pair_ref[1:2, :].astype(jnp.float32), weight
    for d in range(NX):
        weight = jnp.exp2((d_all[d, 8:16, :] - top) * C2)
        total = total + d_all[d, 0:8, :] * weight
        norm = norm + d_all[d, 16:24, :] * weight
    dec_ref[...] = (total / norm)[0:HEADS].astype(jnp.bfloat16)

    for d in (1, 2, 3):
        o_push(d).wait_send()
        t_push(d).wait_send()
        d_push(d).wait_send()
    q_push(2).wait_send()
    q_push(3).wait_send()
    for copy in k_push + v_push:
        copy.wait_send()


def attention(q, k, vt, probe, pair):
    dma = pltpu.SemaphoreType.DMA
    return pl.pallas_call(
        attention_kernel,
        out_shape=(
            jax.ShapeDtypeStruct((ROWS, HEADS * HD), jnp.bfloat16),
            jax.ShapeDtypeStruct((HEADS, HD), jnp.bfloat16),
        ),
        in_specs=[pl.BlockSpec(memory_space=pl.ANY)] * 3
        + [pl.BlockSpec(memory_space=pltpu.VMEM)] * 2,
        out_specs=(pl.BlockSpec(memory_space=pltpu.VMEM),) * 2,
        scratch_shapes=[
            pltpu.VMEM((NX, Q, HD), jnp.bfloat16),
            pltpu.VMEM((NS, KEYS, HD), jnp.bfloat16),
            pltpu.VMEM((NS, HD, KEYS), jnp.bfloat16),
            pltpu.VMEM((NX, HD, Q), jnp.float32),
            pltpu.VMEM((NX, 8, Q), jnp.float32),
            pltpu.VMEM((NX, 8, Q), jnp.float32),
            pltpu.VMEM((2, KEYS, Q), jnp.float32),
            pltpu.VMEM((3, HD, Q), jnp.bfloat16),
            pltpu.VMEM((3, HD, Q), jnp.bfloat16),
            pltpu.VMEM((3, Q // 128, 128), jnp.float32),
            pltpu.VMEM((3, Q // 128, 128), jnp.float32),
            pltpu.VMEM((128, HD), jnp.bfloat16),
            pltpu.VMEM((NX, 24, 128), jnp.float32),
        ] + [dma((3,))] * 13,
        compiler_params=pltpu.CompilerParams(
            collective_id=0, has_side_effects=True, vmem_limit_bytes=60 * 2 ** 20
        ),
        cost_estimate=pl.CostEstimate(
            flops=4 * NX * Q * NS * KEYS * HD, bytes_accessed=4 * 2 ** 20,
            transcendentals=NX * Q * NS * KEYS,
        ),
        name="attention",
    )(q, k, vt, probe, pair)


def projection_kernel(
    a_hbm, w_hbm, y_ref,
    abuf, wbuf, sbuf, rbuf, a_sem, w_sem, a_ss, a_rs, ss, rs,
):
    tp = lax.axis_index("tp")
    z, half = tp // 2, tp % 2

    def at_z(d):
        return {"tp": ((z + d + NZ) % NZ) * 2 + half}

    partner = {"tp": z * 2 + 1 - half}
    order = [4, 3, -3, 2, -2, 1, -1, 0]

    own = pltpu.make_async_copy(a_hbm, abuf.at[half], a_sem)
    own.start()
    blocks = {}
    for n, d in enumerate(order):
        chunk = (z + d + NZ) % NZ
        blocks[d] = pltpu.make_async_copy(w_hbm.at[chunk], wbuf.at[n], w_sem.at[n])
        blocks[d].start()

    signal(partner)
    signal(at_z(1))
    signal(at_z(-1))
    pl.semaphore_wait(pltpu.get_barrier_semaphore(), 3)

    swap = pltpu.make_async_remote_copy(
        src_ref=a_hbm, dst_ref=abuf.at[half], send_sem=a_ss, recv_sem=a_rs,
        device_id=partner, device_id_type=MESH,
    )
    swap.start()
    own.wait()
    swap.wait_recv()

    def term(d):
        n = order.index(d)
        blocks[d].wait()
        return jnp.dot(
            abuf[0], wbuf[n, 0:512, :], preferred_element_type=jnp.float32
        ) + jnp.dot(abuf[1], wbuf[n, 512:1024, :], preferred_element_type=jnp.float32)

    def push(way, step, part):
        n = (way * 4 + step) * 2 + part
        return pltpu.make_async_remote_copy(
            src_ref=sbuf.at[n], dst_ref=rbuf.at[n], send_sem=ss.at[n], recv_sem=rs.at[n],
            device_id=at_z(1 if way == 0 else -1), device_id_type=MESH,
        )

    sent = []

    def send(way, step, part, value):
        sbuf[(way * 4 + step) * 2 + part] = value.astype(jnp.bfloat16)
        copy = push(way, step, part)
        copy.start()
        sent.append(copy)

    def arrived(way, step, part):
        push(way, step, part).wait_recv()
        return rbuf[(way * 4 + step) * 2 + part].astype(jnp.float32)

    def rows(value, part):
        return value[part * 128:(part + 1) * 128]

    y = term(4)
    send(0, 0, 0, rows(y, 0))
    send(1, 0, 1, rows(y, 1))
    right, left = term(3), term(-3)
    send(0, 1, 1, rows(right, 1))
    send(1, 1, 0, rows(left, 0))
    send(0, 1, 0, rows(right, 0) + arrived(0, 0, 0))
    send(1, 1, 1, rows(left, 1) + arrived(1, 0, 1))
    for step in (2, 3):
        right, left = term(4 - step), term(step - 4)
        for first in (0, 1):
            send(0, step, 1 - first, rows(right, 1 - first) + arrived(0, step - 1, 1 - first))
            send(1, step, first, rows(left, first) + arrived(1, step - 1, first))
    y = term(0)
    for part in (1, 0):
        total = rows(y, part) + arrived(0, 3, part) + arrived(1, 3, part)
        y_ref[part * 128:(part + 1) * 128, :] = total.astype(jnp.bfloat16)
    swap.wait_send()
    for copy in sent:
        copy.wait_send()


def projection(a, w):
    dma = pltpu.SemaphoreType.DMA
    return pl.pallas_call(
        projection_kernel,
        out_shape=jax.ShapeDtypeStruct((ROWS, 512), jnp.bfloat16),
        in_specs=[pl.BlockSpec(memory_space=pl.ANY)] * 2,
        out_specs=pl.BlockSpec(memory_space=pltpu.VMEM),
        scratch_shapes=[
            pltpu.VMEM((2, ROWS, 512), jnp.bfloat16),
            pltpu.VMEM((NZ, 1024, 512), jnp.bfloat16),
            pltpu.VMEM((16, 128, 512), jnp.bfloat16),
            pltpu.VMEM((16, 128, 512), jnp.bfloat16),
            dma, dma((NZ,)), dma, dma, dma((16,)), dma((16,)),
        ],
        compiler_params=pltpu.CompilerParams(
            collective_id=1, has_side_effects=True, vmem_limit_bytes=60 * 2 ** 20
        ),
        cost_estimate=pl.CostEstimate(
            flops=2 * ROWS * 1024 * 4096, bytes_accessed=9 * 2 ** 20, transcendentals=0
        ),
        name="projection",
    )(a, w)


def placement_kernel(ids_ref, member_ref, rows_hbm, out_hbm, zeros, sem):
    me = lax.axis_index("inst")
    size = BLK * 2
    zeros[...] = jnp.zeros_like(zeros)

    def take(b, taken):
        mine = ids_ref[member_ref[b]] == me

        @pl.when(mine)
        def _():
            pltpu.make_async_copy(
                rows_hbm.at[pl.ds(b * size, size)], out_hbm.at[pl.ds(taken * size, size)], sem
            ).start()

        return taken + mine.astype(jnp.int32)

    taken = lax.fori_loop(0, 32, take, 0)

    def clear(n, carry):
        pltpu.make_async_copy(zeros, out_hbm.at[pl.ds(n * size, size)], sem).start()
        return carry

    lax.fori_loop(taken, CAP, clear, 0)
    pltpu.make_async_copy(rows_hbm.at[pl.ds(0, CAP * size)], out_hbm, sem).wait()


def placement(ids, members, rows):
    return pl.pallas_call(
        placement_kernel,
        out_shape=jax.ShapeDtypeStruct((CAP * BLK * 2, HD), jnp.bfloat16),
        in_specs=[pl.BlockSpec(memory_space=pltpu.SMEM)] * 2
        + [pl.BlockSpec(memory_space=pl.ANY)],
        out_specs=pl.BlockSpec(memory_space=pl.ANY),
        scratch_shapes=[pltpu.VMEM((BLK * 2, HD), jnp.bfloat16), pltpu.SemaphoreType.DMA],
        compiler_params=pltpu.CompilerParams(vmem_limit_bytes=60 * 2 ** 20),
        name="placement",
    )(ids, members, rows)


def on_device(
    fresh_segment_probes,
    fresh_segment_pairs,
    earlier_stored_pairs,
    emitted_token_probe,
    emitted_token_pair,
    final_projection_weights,
    remaining_instance_ids,
    segment_destination_member,
):
    route = []
    inst_size, tp_size = lax.axis_size("inst"), lax.axis_size("tp")
    for i in range(inst_size):
        for t in range(tp_size):
            core, low = i % 2, t % 2
            route.append((i * tp_size + t, (i - core + low) * tp_size + t - low + core))
    swapped = lax.ppermute(final_projection_weights, ("inst", "tp"), route)
    weights = lax.all_gather(swapped, "inst", axis=0).reshape(NZ, 1024, 512)
    fresh = fresh_segment_pairs.reshape(ROWS * 2, HD)
    moved = lax.all_gather(fresh, "inst", axis=0, tiled=True)

    q = jnp.transpose(fresh_segment_probes, (1, 0, 2)).reshape(Q, HD)
    pairs = jnp.concatenate([earlier_stored_pairs, fresh_segment_pairs], axis=0)[:, :, 0, :]
    a, decode_attention = attention(
        q, pairs[:, 0], pairs[:, 1].T, emitted_token_probe, emitted_token_pair.reshape(2, HD)
    )
    cache = placement(
        remaining_instance_ids, segment_destination_member.reshape(-1), moved
    ).reshape(1, CAP * BLK, 2, 1, HD)
    span_hidden = projection(a, weights)
    return span_hidden, cache, decode_attention


def solution(mesh):
    return jax.shard_map(
        on_device,
        mesh=mesh,
        in_specs=(
            P("inst", "tp", None),
            P("inst", None, "tp", None),
            P("inst", None, "tp", None),
            P("tp", None),
            P(None, "tp", None),
            P("tp", "inst"),
            P(),
            P(),
        ),
        out_specs=(P("inst", "tp"), P("inst", None, None, "tp", None), P("tp", None)),
        check_vma=False,
    )
```

```python
import functools
import jax
import jax.numpy as jnp
from jax import lax
from jax.experimental import pallas as pl
from jax.experimental.pallas import tpu as pltpu
from jax.sharding import PartitionSpec as P

BLK = 128
CAP = 8
ROWS = 256
HEADS = 4
HD = 128
Q = ROWS * HEADS
KEYS = 1280
PIECE = 256
NX = 4
NS = 4
NZ = 8
NEG = -1e30
C2 = float(HD ** -0.5 * 1.4426950408889634)
MESH = pl.DeviceIdType.MESH


def signal(where):
    pl.semaphore_signal(
        pltpu.get_barrier_semaphore(), inc=1, device_id=where, device_id_type=MESH
    )


def fused_kernel(
    q_hbm, fresh_hbm, prefix_hbm, probe_ref, pair_ref, w_hbm,
    y_ref, dec_ref,
    raw, raw_q, stage, qbuf, kbuf, vbuf, acc, m_s, l_s, s_buf,
    o_send, o_recv, st_send, st_recv, qd, d_all, w_all, abuf, sbuf, rbuf,
    loc_sem, q_ss, q_rs, k_ss, k_rs, v_ss, v_rs, o_ss, o_rs, t_ss, t_rs, d_ss, d_rs,
    wy_ss, wy_rs, wx_ss, wx_rs, wf_ss, wf_rs, wc_ss, wc_rs, a_ss, a_rs, r_ss, r_rs,
):
    me = lax.axis_index("inst")
    tp = lax.axis_index("tp")
    x, s = me // NS, me % NS
    far, core = s // 2, s % 2
    z, low = tp // 2, tp % 2
    s1 = s + 1 - 2 * core
    s2 = (s + 2) % NS
    s3 = (s1 + 2) % NS

    def at_x(d):
        return {"inst": ((x + d) % NX) * NS + s}

    def at_s(t):
        return {"inst": x * NS + t}

    def at_w(t):
        return {"inst": x * NS + 2 * t + low, "tp": z * 2 + core}

    def at_z(d, t):
        return {"inst": x * NS + t, "tp": ((z + d + NZ) % NZ) * 2 + low}

    def at_low(t):
        return {"inst": x * NS + t, "tp": z * 2 + 1 - low}

    def remote(src, dst, ss, rs, where):
        return pltpu.make_async_remote_copy(
            src_ref=src, dst_ref=dst, send_sem=ss, recv_sem=rs,
            device_id=where, device_id_type=MESH,
        )

    load = [
        pltpu.make_async_copy(prefix_hbm, raw.at[0:2048], loc_sem.at[0]),
        pltpu.make_async_copy(fresh_hbm, raw.at[2048:2560], loc_sem.at[1]),
        pltpu.make_async_copy(q_hbm, raw_q, loc_sem.at[2]),
    ]
    for copy in load:
        copy.start()

    for d in (1, 2, 3):
        signal(at_x(d))
    signal(at_s(s1))
    signal(at_s(s2))
    signal(at_low(s))
    signal(at_low(s2))
    for d in (1, -1):
        signal(at_z(d, s))
        signal(at_z(d, s2))

    @pl.when(core != low)
    def _():
        signal(at_w(0))
        signal(at_w(1))

    load[0].wait()
    load[1].wait()
    stage[...] = raw[...].astype(jnp.float32)
    kbuf[s] = stage[pl.ds(0, KEYS, stride=2), :].astype(jnp.bfloat16)
    load[2].wait()
    vbuf[s] = jnp.transpose(stage[pl.ds(1, KEYS, stride=2), :]).astype(jnp.bfloat16)
    stage[0:Q] = raw_q[...].astype(jnp.float32)
    for h in range(HEADS):
        qbuf[0, h * ROWS:(h + 1) * ROWS, :] = stage[
            pl.ds(h, ROWS, stride=HEADS), :
        ].astype(jnp.bfloat16)

    pl.semaphore_wait(pltpu.get_barrier_semaphore(), 11 + 2 * ((core + low) % 2))

    def q_push(d):
        return remote(
            qbuf.at[0], qbuf.at[NX - d], q_ss.at[d - 1], q_rs.at[NX - d - 1], at_x(d)
        )

    k_push = [
        remote(kbuf.at[s], kbuf.at[s], k_ss.at[0], k_rs.at[0], at_s(s1)),
        remote(kbuf.at[s], kbuf.at[s], k_ss.at[1], k_rs.at[1], at_s(s2)),
        remote(kbuf.at[s2], kbuf.at[s2], k_ss.at[2], k_rs.at[2], at_s(s1)),
    ]
    v_push = [
        remote(vbuf.at[s], vbuf.at[s], v_ss.at[0], v_rs.at[0], at_s(s1)),
        remote(vbuf.at[s], vbuf.at[s], v_ss.at[1], v_rs.at[1], at_s(s2)),
        remote(vbuf.at[s2], vbuf.at[s2], v_ss.at[2], v_rs.at[2], at_s(s1)),
    ]
    q_push(1).start()
    q_push(3).start()
    k_push[0].start()
    v_push[0].start()
    k_push[1].start()
    v_push[1].start()

    half_rows = pl.ds(pl.multiple_of(core * 512, 512), 512)

    def wy_push(t):
        return remote(
            w_hbm.at[:, t * 256:(t + 1) * 256],
            w_all.at[2 * x + far, pl.ds(pl.multiple_of(low * 512, 512), 512)],
            wy_ss.at[t], wy_rs.at[far], at_w(t),
        )

    def wy_keep(t):
        return pltpu.make_async_copy(
            w_hbm.at[:, t * 256:(t + 1) * 256],
            w_all.at[2 * x + far, pl.ds(pl.multiple_of(low * 512, 512), 512)],
            loc_sem.at[3],
        )

    def each_wy(act, keep):
        for t in (0, 1):
            itself = jnp.logical_and(core == low, far == t)

            @pl.when(itself)
            def _():
                keep(t)

            @pl.when(jnp.logical_not(itself))
            def _():
                act(t)

    def wy_arrival(t):
        piece = w_all.at[2 * x + t, half_rows]
        return remote(piece, piece, wy_ss.at[t], wy_rs.at[t], at_w(t))

    def w_piece(chunk):
        return w_all.at[chunk, half_rows]

    def wx_push(way, g):
        n = way * 2 + g
        piece = w_piece(2 * x + g)
        return remote(piece, piece, wx_ss.at[n], wx_rs.at[n], at_x(1 if way == 0 else 3))

    def wf_push(way):
        origin = (x + (3 if way == 0 else 1)) % NX
        piece = w_piece(2 * origin + way)
        return remote(piece, piece, wf_ss.at[way], wf_rs.at[way], at_x(1 if way == 0 else 3))

    def wc_push(chunk):
        piece = w_piece(chunk)
        return remote(piece, piece, wc_ss.at[chunk], wc_rs.at[chunk], at_s(s1))

    def wc_arrival(chunk):
        piece = w_all.at[chunk, pl.ds(pl.multiple_of((1 - core) * 512, 512), 512)]
        return remote(piece, piece, wc_ss.at[chunk], wc_rs.at[chunk], at_s(s1))

    qd[...] = jnp.zeros_like(qd)
    qd[0:HEADS, :] = probe_ref[...]
    acc[...] = jnp.zeros_like(acc)
    l_s[...] = jnp.zeros_like(l_s)
    m_s[...] = jnp.full(m_s.shape, NEG, jnp.float32)

    key_of = lax.broadcasted_iota(jnp.int32, (PIECE, Q), 0)
    row_of = lax.broadcasted_iota(jnp.int32, (PIECE, Q), 1) % ROWS

    def scores(buf, q, k, j, highest):
        part = lax.dot_general(
            kbuf[k, j * PIECE:(j + 1) * PIECE, :], qbuf[q],
            (((1,), (1,)), ((), ())), preferred_element_type=jnp.float32,
        )
        if j == KEYS // PIECE - 1:
            ahead = ROWS * (((x + q) % NX) * NS + s - (x * NS + k))
            part = jnp.where(key_of - row_of <= ahead, part, NEG)
        s_buf[buf, j * PIECE:(j + 1) * PIECE, :] = part
        return jnp.maximum(highest, jnp.max(part.reshape(PIECE // 8, 8, Q), axis=0))

    lowest = jnp.full((8, Q), NEG, jnp.float32)

    def unit(buf, q, k, highest, following):
        m_old = m_s[q]
        m_new = jnp.maximum(
            m_old, jnp.broadcast_to(jnp.max(highest, axis=0, keepdims=True), (8, Q))
        )
        m_s[q] = m_new
        alpha = jnp.exp2((m_old - m_new) * C2)
        top = m_new[0:1]
        total = acc[q] * alpha[0:1]
        norm = l_s[q] * alpha
        after = lowest
        for j in range(KEYS // PIECE):
            if following is not None:
                after = scores(1 - buf, following[0], following[1], j, after)
            p = jnp.exp2((s_buf[buf, j * PIECE:(j + 1) * PIECE, :] - top) * C2)
            norm = norm + jnp.sum(p.reshape(PIECE // 8, 8, Q), axis=0)
            total = total + jnp.dot(
                vbuf[k, :, j * PIECE:(j + 1) * PIECE], p.astype(jnp.bfloat16),
                preferred_element_type=jnp.float32,
            )
        acc[q] = total
        l_s[q] = norm
        return after

    def q_at(i):
        phase, n = i // 4, i % 4
        near = n + n // 2 - 2 * (n // 3)
        there = 2 - n + 3 * (n // 2) - 2 * (n // 3)
        return near * (1 - phase) + there * phase

    def k_at(i):
        phase = i // 4
        return s * (1 - phase) + s2 * phase, s1 * (1 - phase) + s3 * phase

    def normalised(q, t):
        cols = slice(t * 128, (t + 1) * 128)
        norm = jnp.sum(l_s[q, :, cols], axis=0, keepdims=True)
        return acc[q, :, cols] / norm, m_s[q, 0:1, cols] * C2 + jnp.log2(norm)

    def o_push(d):
        return remote(
            o_send.at[d - 1], o_recv.at[NX - d - 1], o_ss.at[d - 1], o_rs.at[NX - d - 1], at_x(d)
        )

    def t_push(d):
        return remote(
            st_send.at[d - 1], st_recv.at[NX - d - 1], t_ss.at[d - 1], t_rs.at[NX - d - 1], at_x(d)
        )

    highest = lowest
    for j in range(KEYS // PIECE):
        highest = scores(0, 0, s, j, highest)

    def pair(i, highest):
        q = q_at(i)
        ka, kb = k_at(i)

        @pl.when(i == 0)
        def _():
            k_push[0].wait_recv()
            v_push[0].wait_recv()

        @pl.when(i == 4)
        def _():
            k_push[2].wait_recv()
            v_push[2].wait_recv()

        highest = unit(0, q, ka, highest, (q, kb))

        @pl.when(i == 0)
        def _():
            q_push(1).wait_send()
            q_push(2).start()
            q_push(3).wait_recv()

        @pl.when(i == 1)
        def _():
            q_push(1).wait_recv()

        @pl.when(i == 2)
        def _():
            q_push(2).wait_recv()

        @pl.when(i == 3)
        def _():
            k_push[1].wait_recv()
            k_push[2].start()
            v_push[1].wait_recv()
            v_push[2].start()

        highest = unit(1, q, kb, highest, (q_at(i + 1), k_at(i + 1)[0]))

        @pl.when(i == 0)
        def _():
            each_wy(lambda t: wy_push(t).start(), lambda t: wy_keep(t).start())

        @pl.when(i == 2)
        def _():
            each_wy(lambda t: wy_arrival(t).wait_recv(), lambda t: wy_keep(t).wait())
            for g in (0, 1):
                wx_push(0, g).start()
                wx_push(1, g).start()
            wc_push(2 * x).start()
            wc_push(2 * x + 1).start()

        @pl.when(i >= 4)
        def _():
            for t in range(Q // 128):
                o, lse = normalised(q, t)
                o_send[q - 1, :, t * 128:(t + 1) * 128] = o.astype(jnp.bfloat16)
                st_send[q - 1, t:t + 1, :] = lse
            o_push(q).start()
            t_push(q).start()

        @pl.when(i == 6)
        def _():
            for way in (0, 1):
                origin = (x + (3 if way == 0 else 1)) % NX
                wx_push(way, way).wait_recv()
                wf_push(way).start()
                wx_push(way, 1 - way).wait_recv()
                wc_push(2 * origin).start()
                wc_push(2 * origin + 1).start()

        return highest

    highest = lax.fori_loop(0, 7, pair, highest)
    highest = unit(0, 0, s2, highest, (0, s3))
    unit(1, 0, s3, highest, None)

    dm = jnp.full((1, 128), NEG, jnp.float32)
    dl = jnp.zeros((1, 128), jnp.float32)
    da = jnp.zeros((HD, 128), jnp.float32)
    for k in range(NS):
        part = lax.dot_general(
            kbuf[k], qd[...], (((1,), (1,)), ((), ())), preferred_element_type=jnp.float32
        )
        new = jnp.maximum(dm, jnp.max(part, axis=0, keepdims=True))
        alpha = jnp.exp2((dm - new) * C2)
        p = jnp.exp2((part - new) * C2)
        dl = dl * alpha + jnp.sum(p, axis=0, keepdims=True)
        da = da * alpha + jnp.dot(
            vbuf[k], p.astype(jnp.bfloat16), preferred_element_type=jnp.float32
        )
        dm = new
    d_all[x, 0:8, :] = jnp.transpose(da)[0:8]
    d_all[x, 8:16, :] = jnp.transpose(jnp.broadcast_to(dm, (128, 128)))[0:8]
    d_all[x, 16:24, :] = jnp.transpose(jnp.broadcast_to(dl, (128, 128)))[0:8]

    def d_push(d):
        return remote(d_all.at[x], d_all.at[x], d_ss.at[d - 1], d_rs.at[NX - d - 1], at_x(d))

    for d in (1, 2, 3):
        d_push(d).start()

    for d in (1, 2, 3):
        o_push(d).wait_recv()
        t_push(d).wait_recv()
    for t in range(Q // 128):
        cols = slice(t * 128, (t + 1) * 128)
        o, lse = normalised(0, t)
        rest = [st_recv[d, t:t + 1, :] for d in range(3)]
        top = functools.reduce(jnp.maximum, rest, lse)
        weight = jnp.exp2(lse - top)
        total, norm = o * weight, weight
        for d in range(3):
            weight = jnp.exp2(rest[d] - top)
            total = total + o_recv[d, :, cols].astype(jnp.float32) * weight
            norm = norm + weight
        h, r = t // 2, (t % 2) * 128
        abuf[0, low, r:r + 128, h * HD:(h + 1) * HD] = jnp.transpose(total / norm).astype(
            jnp.bfloat16
        )

    a_push = [
        remote(abuf.at[0, low], abuf.at[0, low], a_ss.at[0], a_rs.at[0], at_low(s)),
        remote(abuf.at[0, low], abuf.at[1, low], a_ss.at[1], a_rs.at[1], at_low(s2)),
        remote(abuf.at[0, low], abuf.at[1, low], a_ss.at[2], a_rs.at[2], at_s(s2)),
    ]
    for copy in a_push:
        copy.start()

    for way in (0, 1):
        wf_push(way).wait_recv()
        wc_push(2 * ((x + 2) % NX) + way).start()

    for d in (1, 2, 3):
        d_push(d).wait_recv()
    query = qd[0:8, :].astype(jnp.float32)
    last = jnp.sum(query * pair_ref[0:1, :].astype(jnp.float32), axis=1, keepdims=True)
    last = jnp.broadcast_to(last, (8, HD))
    top = last
    for d in range(NX):
        top = jnp.maximum(top, d_all[d, 8:16, :])
    weight = jnp.exp2((last - top) * C2)
    total, norm = weight * pair_ref[1:2, :].astype(jnp.float32), weight
    for d in range(NX):
        weight = jnp.exp2((d_all[d, 8:16, :] - top) * C2)
        total = total + d_all[d, 0:8, :] * weight
        norm = norm + d_all[d, 16:24, :] * weight
    dec_ref[...] = (total / norm)[0:HEADS].astype(jnp.bfloat16)

    for chunk in range(NZ):
        wc_arrival(chunk).wait_recv()

    def term(d, r):
        chunk = (z + d + NZ) % NZ
        return jnp.dot(
            abuf[r, 0], w_all[chunk, 0:512, :], preferred_element_type=jnp.float32
        ) + jnp.dot(abuf[r, 1], w_all[chunk, 512:1024, :], preferred_element_type=jnp.float32)

    def push(way, step, r):
        n = (way * 4 + step) * 2 + r
        return remote(
            sbuf.at[n], rbuf.at[n], r_ss.at[n], r_rs.at[n],
            at_z(1 if way == 0 else -1, s2 if (step == 3 and r == 1) else s),
        )

    sent = []

    def send(way, step, r, value):
        sbuf[(way * 4 + step) * 2 + r] = value.astype(jnp.bfloat16)
        copy = push(way, step, r)
        copy.start()
        sent.append(copy)

    def arrived(way, step, r):
        push(way, step, r).wait_recv()
        return rbuf[(way * 4 + step) * 2 + r].astype(jnp.float32)

    a_push[0].wait_recv()
    send(0, 0, 0, term(4, 0))
    send(1, 1, 0, term(-3, 0))
    a_push[1].wait_recv()
    a_push[2].wait_recv()
    send(1, 0, 1, term(4, 1))
    send(0, 1, 1, term(3, 1))
    send(0, 1, 0, term(3, 0) + arrived(0, 0, 0))
    send(1, 1, 1, term(-3, 1) + arrived(1, 0, 1))
    sbuf[16] = term(0, 1).astype(jnp.bfloat16)
    other = remote(sbuf.at[16], rbuf.at[16], r_ss.at[16], r_rs.at[16], at_s(s2))
    other.start()
    for step in (2, 3):
        send(1, step, 0, term(step - 4, 0) + arrived(1, step - 1, 0))
        send(0, step, 1, term(4 - step, 1) + arrived(0, step - 1, 1))
        send(0, step, 0, term(4 - step, 0) + arrived(0, step - 1, 0))
        send(1, step, 1, term(step - 4, 1) + arrived(1, step - 1, 1))
    total = term(0, 0) + arrived(1, 3, 0) + arrived(0, 3, 0)
    y_ref[:, pl.ds(pl.multiple_of(far * 256, 256), 256)] = total.astype(jnp.bfloat16)
    other.wait_recv()
    total = rbuf[16].astype(jnp.float32) + arrived(0, 3, 1) + arrived(1, 3, 1)
    y_ref[:, pl.ds(pl.multiple_of((1 - far) * 256, 256), 256)] = total.astype(jnp.bfloat16)

    other.wait_send()
    for copy in sent + a_push + k_push + v_push:
        copy.wait_send()
    for d in (1, 2, 3):
        o_push(d).wait_send()
        t_push(d).wait_send()
        d_push(d).wait_send()
    q_push(2).wait_send()
    q_push(3).wait_send()
    each_wy(lambda t: wy_push(t).wait_send(), lambda t: None)
    for way in (0, 1):
        wx_push(way, 0).wait_send()
        wx_push(way, 1).wait_send()
        wf_push(way).wait_send()
    for chunk in range(NZ):
        wc_push(chunk).wait_send()


def fused(q, fresh, prefix, probe, pair, w):
    dma = pltpu.SemaphoreType.DMA
    bf16, f32 = jnp.bfloat16, jnp.float32
    return pl.pallas_call(
        fused_kernel,
        out_shape=(
            jax.ShapeDtypeStruct((ROWS, 512), bf16),
            jax.ShapeDtypeStruct((HEADS, HD), bf16),
        ),
        in_specs=[pl.BlockSpec(memory_space=pl.ANY)] * 3
        + [pl.BlockSpec(memory_space=pltpu.VMEM)] * 2
        + [pl.BlockSpec(memory_space=pl.ANY)],
        out_specs=(pl.BlockSpec(memory_space=pltpu.VMEM),) * 2,
        scratch_shapes=[
            pltpu.VMEM((2 * KEYS, HD), bf16),
            pltpu.VMEM((Q, HD), bf16),
            pltpu.VMEM((2 * KEYS, HD), f32),
            pltpu.VMEM((NX, Q, HD), bf16),
            pltpu.VMEM((NS, KEYS, HD), bf16),
            pltpu.VMEM((NS, HD, KEYS), bf16),
            pltpu.VMEM((NX, HD, Q), f32),
            pltpu.VMEM((NX, 8, Q), f32),
            pltpu.VMEM((NX, 8, Q), f32),
            pltpu.VMEM((2, KEYS, Q), f32),
            pltpu.VMEM((3, HD, Q), bf16),
            pltpu.VMEM((3, HD, Q), bf16),
            pltpu.VMEM((3, Q // 128, 128), f32),
            pltpu.VMEM((3, Q // 128, 128), f32),
            pltpu.VMEM((128, HD), bf16),
            pltpu.VMEM((NX, 24, 128), f32),
            pltpu.VMEM((NZ, 1024, 256), bf16),
            pltpu.VMEM((2, 2, ROWS, 512), bf16),
            pltpu.VMEM((17, ROWS, 256), bf16),
            pltpu.VMEM((17, ROWS, 256), bf16),
            dma((4,)),
        ] + [dma((3,))] * 12 + [
            dma((2,)), dma((2,)), dma((4,)), dma((4,)), dma((2,)), dma((2,)),
            dma((NZ,)), dma((NZ,)), dma((3,)), dma((3,)), dma((17,)), dma((17,)),
        ],
        compiler_params=pltpu.CompilerParams(
            collective_id=0, has_side_effects=True, vmem_limit_bytes=60 * 2 ** 20
        ),
        cost_estimate=pl.CostEstimate(
            flops=4 * NX * Q * NS * KEYS * HD, bytes_accessed=4 * 2 ** 20,
            transcendentals=NX * Q * NS * KEYS,
        ),
        name="attention_and_projection",
    )(q, fresh, prefix, probe, pair, w)


def placement_kernel(ids_ref, member_ref, rows_hbm, out_hbm, zeros, sem):
    me = lax.axis_index("inst")
    size = BLK * 2
    zeros[...] = jnp.zeros_like(zeros)

    def take(b, taken):
        mine = ids_ref[member_ref[b]] == me

        @pl.when(mine)
        def _():
            pltpu.make_async_copy(
                rows_hbm.at[pl.ds(b * size, size)], out_hbm.at[pl.ds(taken * size, size)], sem
            ).start()

        return taken + mine.astype(jnp.int32)

    taken = lax.fori_loop(0, 32, take, 0)

    def clear(n, carry):
        pltpu.make_async_copy(zeros, out_hbm.at[pl.ds(n * size, size)], sem).start()
        return carry

    lax.fori_loop(taken, CAP, clear, 0)
    pltpu.make_async_copy(rows_hbm.at[pl.ds(0, CAP * size)], out_hbm, sem).wait()


def placement(ids, members, rows):
    return pl.pallas_call(
        placement_kernel,
        out_shape=jax.ShapeDtypeStruct((CAP * BLK * 2, HD), jnp.bfloat16),
        in_specs=[pl.BlockSpec(memory_space=pltpu.SMEM)] * 2
        + [pl.BlockSpec(memory_space=pl.ANY)],
        out_specs=pl.BlockSpec(memory_space=pl.ANY),
        scratch_shapes=[pltpu.VMEM((BLK * 2, HD), jnp.bfloat16), pltpu.SemaphoreType.DMA],
        compiler_params=pltpu.CompilerParams(vmem_limit_bytes=60 * 2 ** 20),
        name="placement",
    )(ids, members, rows)


def on_device(
    fresh_segment_probes,
    fresh_segment_pairs,
    earlier_stored_pairs,
    emitted_token_probe,
    emitted_token_pair,
    final_projection_weights,
    remaining_instance_ids,
    segment_destination_member,
):
    fresh = fresh_segment_pairs.reshape(ROWS * 2, HD)
    moved = lax.all_gather(fresh, "inst", axis=0, tiled=True)
    span_hidden, decode_attention = fused(
        fresh_segment_probes.reshape(Q, HD),
        fresh,
        earlier_stored_pairs.reshape(4 * ROWS * 2, HD),
        emitted_token_probe,
        emitted_token_pair.reshape(2, HD),
        final_projection_weights,
    )
    cache = placement(
        remaining_instance_ids, segment_destination_member.reshape(-1), moved
    ).reshape(1, CAP * BLK, 2, 1, HD)
    return span_hidden, cache, decode_attention


def solution(mesh):
    return jax.shard_map(
        on_device,
        mesh=mesh,
        in_specs=(
            P("inst", "tp", None),
            P("inst", None, "tp", None),
            P("inst", None, "tp", None),
            P("tp", None),
            P(None, "tp", None),
            P("tp", "inst"),
            P(),
            P(),
        ),
        out_specs=(P("inst", "tp"), P("inst", None, None, "tp", None), P("tp", None)),
        check_vma=False,
    )
```

```python
import functools
import jax
import jax.numpy as jnp
from jax import lax
from jax.experimental import pallas as pl
from jax.experimental.pallas import tpu as pltpu
from jax.sharding import PartitionSpec as P

BLK = 128
CAP = 8
ROWS = 256
HEADS = 4
HD = 128
Q = ROWS * HEADS
KEYS = 1280
PIECE = 256
NX = 4
NS = 4
NZ = 8
NEG = -1e30
C2 = float(HD ** -0.5 * 1.4426950408889634)
MESH = pl.DeviceIdType.MESH


def signal(where):
    pl.semaphore_signal(
        pltpu.get_barrier_semaphore(), inc=1, device_id=where, device_id_type=MESH
    )


def fused_kernel(
    q_hbm, fresh_hbm, prefix_hbm, probe_ref, pair_ref, w_hbm,
    y_ref, dec_ref, moved,
    raw, raw_q, stage, qbuf, kbuf, vbuf, acc, m_s, l_s, s_buf,
    o_send, o_recv, st_send, st_recv, qd, d_all, w_all, abuf, sbuf, rbuf,
    loc_sem, q_ss, q_rs, k_ss, k_rs, v_ss, v_rs, o_ss, o_rs, t_ss, t_rs, d_ss, d_rs,
    wy_ss, wy_rs, wx_ss, wx_rs, wf_ss, wf_rs, wc_ss, wc_rs, a_ss, a_rs, r_ss, r_rs,
    cy_ss, cy_rs, cx_ss, cx_rs, cc_ss, cc_rs,
):
    me = lax.axis_index("inst")
    tp = lax.axis_index("tp")
    x, s = me // NS, me % NS
    far, core = s // 2, s % 2
    z, low = tp // 2, tp % 2
    s1 = s + 1 - 2 * core
    s2 = (s + 2) % NS
    s3 = (s1 + 2) % NS

    def at_x(d):
        return {"inst": ((x + d) % NX) * NS + s}

    def at_s(t):
        return {"inst": x * NS + t}

    def at_w(t):
        return {"inst": x * NS + 2 * t + low, "tp": z * 2 + core}

    def at_z(d, t):
        return {"inst": x * NS + t, "tp": ((z + d + NZ) % NZ) * 2 + low}

    def at_low(t):
        return {"inst": x * NS + t, "tp": z * 2 + 1 - low}

    def remote(src, dst, ss, rs, where):
        return pltpu.make_async_remote_copy(
            src_ref=src, dst_ref=dst, send_sem=ss, recv_sem=rs,
            device_id=where, device_id_type=MESH,
        )

    load = [
        pltpu.make_async_copy(prefix_hbm, raw.at[0:2048], loc_sem.at[0]),
        pltpu.make_async_copy(fresh_hbm, raw.at[2048:2560], loc_sem.at[1]),
        pltpu.make_async_copy(q_hbm, raw_q, loc_sem.at[2]),
    ]
    for copy in load:
        copy.start()

    for d in (1, 2, 3):
        signal(at_x(d))
    signal(at_s(s1))
    signal(at_s(s2))
    signal(at_low(s))
    signal(at_low(s2))
    for d in (1, -1):
        signal(at_z(d, s))
        signal(at_z(d, s2))

    @pl.when(core != low)
    def _():
        signal(at_w(0))
        signal(at_w(1))

    load[0].wait()
    load[1].wait()
    stage[...] = raw[...].astype(jnp.float32)
    kbuf[s] = stage[pl.ds(0, KEYS, stride=2), :].astype(jnp.bfloat16)
    load[2].wait()
    vbuf[s] = jnp.transpose(stage[pl.ds(1, KEYS, stride=2), :]).astype(jnp.bfloat16)
    stage[0:Q] = raw_q[...].astype(jnp.float32)
    for h in range(HEADS):
        qbuf[0, h * ROWS:(h + 1) * ROWS, :] = stage[
            pl.ds(h, ROWS, stride=HEADS), :
        ].astype(jnp.bfloat16)

    pl.semaphore_wait(pltpu.get_barrier_semaphore(), 11 + 2 * ((core + low) % 2))

    def q_push(d):
        return remote(
            qbuf.at[0], qbuf.at[NX - d], q_ss.at[d - 1], q_rs.at[NX - d - 1], at_x(d)
        )

    k_push = [
        remote(kbuf.at[s], kbuf.at[s], k_ss.at[0], k_rs.at[0], at_s(s1)),
        remote(kbuf.at[s], kbuf.at[s], k_ss.at[1], k_rs.at[1], at_s(s2)),
        remote(kbuf.at[s2], kbuf.at[s2], k_ss.at[2], k_rs.at[2], at_s(s1)),
    ]
    v_push = [
        remote(vbuf.at[s], vbuf.at[s], v_ss.at[0], v_rs.at[0], at_s(s1)),
        remote(vbuf.at[s], vbuf.at[s], v_ss.at[1], v_rs.at[1], at_s(s2)),
        remote(vbuf.at[s2], vbuf.at[s2], v_ss.at[2], v_rs.at[2], at_s(s1)),
    ]
    half_rows = pl.ds(pl.multiple_of(core * 512, 512), 512)

    def wy_push(t):
        return remote(
            w_hbm.at[:, t * 256:(t + 1) * 256],
            w_all.at[2 * x + far, pl.ds(pl.multiple_of(low * 512, 512), 512)],
            wy_ss.at[t], wy_rs.at[far], at_w(t),
        )

    def wy_keep(t):
        return pltpu.make_async_copy(
            w_hbm.at[:, t * 256:(t + 1) * 256],
            w_all.at[2 * x + far, pl.ds(pl.multiple_of(low * 512, 512), 512)],
            loc_sem.at[3],
        )

    def each_wy(act, keep):
        for t in (0, 1):
            itself = jnp.logical_and(core == low, far == t)

            @pl.when(itself)
            def _():
                keep(t)

            @pl.when(jnp.logical_not(itself))
            def _():
                act(t)

    def wy_arrival(t):
        piece = w_all.at[2 * x + t, half_rows]
        return remote(piece, piece, wy_ss.at[t], wy_rs.at[t], at_w(t))

    def w_piece(chunk):
        return w_all.at[chunk, half_rows]

    def wx_push(way, g):
        n = way * 2 + g
        piece = w_piece(2 * x + g)
        return remote(piece, piece, wx_ss.at[n], wx_rs.at[n], at_x(1 if way == 0 else 3))

    def wf_push(way):
        origin = (x + (3 if way == 0 else 1)) % NX
        piece = w_piece(2 * origin + way)
        return remote(piece, piece, wf_ss.at[way], wf_rs.at[way], at_x(1 if way == 0 else 3))

    def wc_push(chunk):
        piece = w_piece(chunk)
        return remote(piece, piece, wc_ss.at[chunk], wc_rs.at[chunk], at_s(s1))

    def wc_arrival(chunk):
        piece = w_all.at[chunk, pl.ds(pl.multiple_of((1 - core) * 512, 512), 512)]
        return remote(piece, piece, wc_ss.at[chunk], wc_rs.at[chunk], at_s(s1))

    each_wy(lambda t: wy_push(t).start(), lambda t: wy_keep(t).start())
    q_push(1).start()
    q_push(3).start()
    k_push[0].start()
    v_push[0].start()
    k_push[1].start()
    v_push[1].start()

    fresh = raw.at[2048:2560]

    def cy_push():
        return remote(fresh, moved.at[me], cy_ss, cy_rs, at_s(s2))

    def cx_push(n, d):
        src = fresh if n == 0 else moved.at[x * NS + s2]
        dst = moved.at[me] if n == 0 else moved.at[x * NS + s2]
        i = n * 3 + d - 1
        return remote(src, dst, cx_ss.at[i], cx_rs.at[n * 3 + NX - d - 1], at_x(d))

    def cc_push(d, n):
        block = moved.at[((x + d) % NX) * NS + (s, s2)[n]]
        i = d * 2 + n
        return remote(block, block, cc_ss.at[i], cc_rs.at[i], at_s(s1))

    moved_own = pltpu.make_async_copy(fresh, moved.at[me], loc_sem.at[4])

    qd[...] = jnp.zeros_like(qd)
    qd[0:HEADS, :] = probe_ref[...]
    acc[...] = jnp.zeros_like(acc)
    l_s[...] = jnp.zeros_like(l_s)
    m_s[...] = jnp.full(m_s.shape, NEG, jnp.float32)

    key_of = lax.broadcasted_iota(jnp.int32, (PIECE, Q), 0)
    row_of = lax.broadcasted_iota(jnp.int32, (PIECE, Q), 1) % ROWS

    def scores(buf, q, k, j, highest):
        part = lax.dot_general(
            kbuf[k, j * PIECE:(j + 1) * PIECE, :], qbuf[q],
            (((1,), (1,)), ((), ())), preferred_element_type=jnp.float32,
        )
        if j == KEYS // PIECE - 1:
            ahead = ROWS * (((x + q) % NX) * NS + s - (x * NS + k))
            part = jnp.where(key_of - row_of <= ahead, part, NEG)
        s_buf[buf, j * PIECE:(j + 1) * PIECE, :] = part
        return jnp.maximum(highest, jnp.max(part.reshape(PIECE // 8, 8, Q), axis=0))

    lowest = jnp.full((8, Q), NEG, jnp.float32)

    def unit(buf, q, k, highest, following):
        m_old = m_s[q]
        m_new = jnp.maximum(
            m_old, jnp.broadcast_to(jnp.max(highest, axis=0, keepdims=True), (8, Q))
        )
        m_s[q] = m_new
        alpha = jnp.exp2((m_old - m_new) * C2)
        top = m_new[0:1]
        total = acc[q] * alpha[0:1]
        norm = l_s[q] * alpha
        after = lowest
        for j in range(KEYS // PIECE):
            if following is not None:
                after = scores(1 - buf, following[0], following[1], j, after)
            p = jnp.exp2((s_buf[buf, j * PIECE:(j + 1) * PIECE, :] - top) * C2)
            norm = norm + jnp.sum(p.reshape(PIECE // 8, 8, Q), axis=0)
            total = total + jnp.dot(
                vbuf[k, :, j * PIECE:(j + 1) * PIECE], p.astype(jnp.bfloat16),
                preferred_element_type=jnp.float32,
            )
        acc[q] = total
        l_s[q] = norm
        return after

    def q_at(i):
        phase, n = i // 4, i % 4
        near = n + n // 2 - 2 * (n // 3)
        there = 2 - n + 3 * (n // 2) - 2 * (n // 3)
        return near * (1 - phase) + there * phase

    def k_at(i):
        phase = i // 4
        return s * (1 - phase) + s2 * phase, s1 * (1 - phase) + s3 * phase

    def normalised(q, t):
        cols = slice(t * 128, (t + 1) * 128)
        norm = jnp.sum(l_s[q, :, cols], axis=0, keepdims=True)
        return acc[q, :, cols] / norm, m_s[q, 0:1, cols] * C2 + jnp.log2(norm)

    def o_push(d):
        return remote(
            o_send.at[d - 1], o_recv.at[NX - d - 1], o_ss.at[d - 1], o_rs.at[NX - d - 1], at_x(d)
        )

    def t_push(d):
        return remote(
            st_send.at[d - 1], st_recv.at[NX - d - 1], t_ss.at[d - 1], t_rs.at[NX - d - 1], at_x(d)
        )

    highest = lowest
    for j in range(KEYS // PIECE):
        highest = scores(0, 0, s, j, highest)

    def pair(i, highest):
        q = q_at(i)
        ka, kb = k_at(i)

        @pl.when(i == 0)
        def _():
            k_push[0].wait_recv()
            v_push[0].wait_recv()

        @pl.when(i == 4)
        def _():
            k_push[2].wait_recv()
            v_push[2].wait_recv()

        highest = unit(0, q, ka, highest, (q, kb))

        @pl.when(i == 0)
        def _():
            q_push(1).wait_send()
            q_push(2).start()
            q_push(3).wait_recv()

        @pl.when(i == 1)
        def _():
            q_push(1).wait_recv()

        @pl.when(i == 2)
        def _():
            q_push(2).wait_recv()

        @pl.when(i == 3)
        def _():
            k_push[1].wait_recv()
            k_push[2].start()
            v_push[1].wait_recv()
            v_push[2].start()

        highest = unit(1, q, kb, highest, (q_at(i + 1), k_at(i + 1)[0]))

        @pl.when(i == 1)
        def _():
            each_wy(lambda t: wy_arrival(t).wait_recv(), lambda t: wy_keep(t).wait())
            for g in (0, 1):
                wx_push(0, g).start()
                wx_push(1, g).start()
            wc_push(2 * x).start()
            wc_push(2 * x + 1).start()

        @pl.when(i >= 4)
        def _():
            for t in range(Q // 128):
                o, lse = normalised(q, t)
                o_send[q - 1, :, t * 128:(t + 1) * 128] = o.astype(jnp.bfloat16)
                st_send[q - 1, t:t + 1, :] = lse
            o_push(q).start()
            t_push(q).start()

        @pl.when(i == 4)
        def _():
            cy_push().start()
            moved_own.start()

        @pl.when(i == 5)
        def _():
            for way in (0, 1):
                origin = (x + (3 if way == 0 else 1)) % NX
                wx_push(way, way).wait_recv()
                wf_push(way).start()
                wx_push(way, 1 - way).wait_recv()
                wc_push(2 * origin).start()
                wc_push(2 * origin + 1).start()

        return highest

    highest = lax.fori_loop(0, 7, pair, highest)
    highest = unit(0, 0, s2, highest, (0, s3))
    unit(1, 0, s3, highest, None)

    dm = jnp.full((1, 128), NEG, jnp.float32)
    dl = jnp.zeros((1, 128), jnp.float32)
    da = jnp.zeros((HD, 128), jnp.float32)
    for k in range(NS):
        part = lax.dot_general(
            kbuf[k], qd[...], (((1,), (1,)), ((), ())), preferred_element_type=jnp.float32
        )
        new = jnp.maximum(dm, jnp.max(part, axis=0, keepdims=True))
        alpha = jnp.exp2((dm - new) * C2)
        p = jnp.exp2((part - new) * C2)
        dl = dl * alpha + jnp.sum(p, axis=0, keepdims=True)
        da = da * alpha + jnp.dot(
            vbuf[k], p.astype(jnp.bfloat16), preferred_element_type=jnp.float32
        )
        dm = new
    d_all[x, 0:8, :] = jnp.transpose(da)[0:8]
    d_all[x, 8:16, :] = jnp.transpose(jnp.broadcast_to(dm, (128, 128)))[0:8]
    d_all[x, 16:24, :] = jnp.transpose(jnp.broadcast_to(dl, (128, 128)))[0:8]

    def d_push(d):
        return remote(d_all.at[x], d_all.at[x], d_ss.at[d - 1], d_rs.at[NX - d - 1], at_x(d))

    for d in (1, 2, 3):
        d_push(d).start()

    for d in (1, 2, 3):
        o_push(d).wait_recv()
        t_push(d).wait_recv()
    for t in range(Q // 128):
        cols = slice(t * 128, (t + 1) * 128)
        o, lse = normalised(0, t)
        rest = [st_recv[d, t:t + 1, :] for d in range(3)]
        top = functools.reduce(jnp.maximum, rest, lse)
        weight = jnp.exp2(lse - top)
        total, norm = o * weight, weight
        for d in range(3):
            weight = jnp.exp2(rest[d] - top)
            total = total + o_recv[d, :, cols].astype(jnp.float32) * weight
            norm = norm + weight
        h, r = t // 2, (t % 2) * 128
        abuf[0, low, r:r + 128, h * HD:(h + 1) * HD] = jnp.transpose(total / norm).astype(
            jnp.bfloat16
        )

    a_push = [
        remote(abuf.at[0, low], abuf.at[0, low], a_ss.at[0], a_rs.at[0], at_low(s)),
        remote(abuf.at[0, low], abuf.at[1, low], a_ss.at[1], a_rs.at[1], at_low(s2)),
        remote(abuf.at[0, low], abuf.at[1, low], a_ss.at[2], a_rs.at[2], at_s(s2)),
    ]
    for copy in a_push:
        copy.start()
    cy_push().wait_recv()
    moved_own.wait()
    for n in (0, 1):
        for d in (1, 3, 2):
            cx_push(n, d).start()
        cc_push(0, n).start()

    for way in (0, 1):
        wf_push(way).wait_recv()
        wc_push(2 * ((x + 2) % NX) + way).start()

    for d in (1, 2, 3):
        d_push(d).wait_recv()
    query = qd[0:8, :].astype(jnp.float32)
    last = jnp.sum(query * pair_ref[0:1, :].astype(jnp.float32), axis=1, keepdims=True)
    last = jnp.broadcast_to(last, (8, HD))
    top = last
    for d in range(NX):
        top = jnp.maximum(top, d_all[d, 8:16, :])
    weight = jnp.exp2((last - top) * C2)
    total, norm = weight * pair_ref[1:2, :].astype(jnp.float32), weight
    for d in range(NX):
        weight = jnp.exp2((d_all[d, 8:16, :] - top) * C2)
        total = total + d_all[d, 0:8, :] * weight
        norm = norm + d_all[d, 16:24, :] * weight
    dec_ref[...] = (total / norm)[0:HEADS].astype(jnp.bfloat16)

    for chunk in range(NZ):
        wc_arrival(chunk).wait_recv()

    def term(d, r):
        chunk = (z + d + NZ) % NZ
        return jnp.dot(
            abuf[r, 0], w_all[chunk, 0:512, :], preferred_element_type=jnp.float32
        ) + jnp.dot(abuf[r, 1], w_all[chunk, 512:1024, :], preferred_element_type=jnp.float32)

    def push(way, step, r):
        n = (way * 4 + step) * 2 + r
        return remote(
            sbuf.at[n], rbuf.at[n], r_ss.at[n], r_rs.at[n],
            at_z(1 if way == 0 else -1, s2 if (step == 3 and r == 1) else s),
        )

    sent = []

    def send(way, step, r, value):
        sbuf[(way * 4 + step) * 2 + r] = value.astype(jnp.bfloat16)
        copy = push(way, step, r)
        copy.start()
        sent.append(copy)

    def arrived(way, step, r):
        push(way, step, r).wait_recv()
        return rbuf[(way * 4 + step) * 2 + r].astype(jnp.float32)

    a_push[0].wait_recv()
    send(0, 0, 0, term(4, 0))
    send(1, 1, 0, term(-3, 0))
    a_push[1].wait_recv()
    a_push[2].wait_recv()
    send(1, 0, 1, term(4, 1))
    send(0, 1, 1, term(3, 1))
    send(0, 1, 0, term(3, 0) + arrived(0, 0, 0))
    send(1, 1, 1, term(-3, 1) + arrived(1, 0, 1))
    sbuf[16] = term(0, 1).astype(jnp.bfloat16)
    other = remote(sbuf.at[16], rbuf.at[16], r_ss.at[16], r_rs.at[16], at_s(s2))
    other.start()
    for step in (2, 3):
        send(1, step, 0, term(step - 4, 0) + arrived(1, step - 1, 0))
        send(0, step, 1, term(4 - step, 1) + arrived(0, step - 1, 1))
        send(0, step, 0, term(4 - step, 0) + arrived(0, step - 1, 0))
        send(1, step, 1, term(step - 4, 1) + arrived(1, step - 1, 1))
    for d in (1, 3, 2):
        for n in (0, 1):
            cx_push(n, NX - d).wait_recv()
            cc_push(d, n).start()
    total = term(0, 0) + arrived(1, 3, 0) + arrived(0, 3, 0)
    y_ref[:, pl.ds(pl.multiple_of(far * 256, 256), 256)] = total.astype(jnp.bfloat16)
    other.wait_recv()
    total = rbuf[16].astype(jnp.float32) + arrived(0, 3, 1) + arrived(1, 3, 1)
    y_ref[:, pl.ds(pl.multiple_of((1 - far) * 256, 256), 256)] = total.astype(jnp.bfloat16)

    cy_push().wait_send()
    for n in (0, 1):
        for d in (1, 2, 3):
            cx_push(n, d).wait_send()
        for d in range(NX):
            cc_push(d, n).wait_send()
            cc_push(d, n).wait_recv()
    other.wait_send()
    for copy in sent + a_push + k_push + v_push:
        copy.wait_send()
    for d in (1, 2, 3):
        o_push(d).wait_send()
        t_push(d).wait_send()
        d_push(d).wait_send()
    q_push(2).wait_send()
    q_push(3).wait_send()
    each_wy(lambda t: wy_push(t).wait_send(), lambda t: None)
    for way in (0, 1):
        wx_push(way, 0).wait_send()
        wx_push(way, 1).wait_send()
        wf_push(way).wait_send()
    for chunk in range(NZ):
        wc_push(chunk).wait_send()


def fused(q, fresh, prefix, probe, pair, w):
    dma = pltpu.SemaphoreType.DMA
    bf16, f32 = jnp.bfloat16, jnp.float32
    return pl.pallas_call(
        fused_kernel,
        out_shape=(
            jax.ShapeDtypeStruct((ROWS, 512), bf16),
            jax.ShapeDtypeStruct((HEADS, HD), bf16),
            jax.ShapeDtypeStruct((NX * NS, 2 * ROWS, HD), bf16),
        ),
        in_specs=[pl.BlockSpec(memory_space=pl.ANY)] * 3
        + [pl.BlockSpec(memory_space=pltpu.VMEM)] * 2
        + [pl.BlockSpec(memory_space=pl.ANY)],
        out_specs=(pl.BlockSpec(memory_space=pltpu.VMEM),) * 2
        + (pl.BlockSpec(memory_space=pl.ANY),),
        scratch_shapes=[
            pltpu.VMEM((2 * KEYS, HD), bf16),
            pltpu.VMEM((Q, HD), bf16),
            pltpu.VMEM((2 * KEYS, HD), f32),
            pltpu.VMEM((NX, Q, HD), bf16),
            pltpu.VMEM((NS, KEYS, HD), bf16),
            pltpu.VMEM((NS, HD, KEYS), bf16),
            pltpu.VMEM((NX, HD, Q), f32),
            pltpu.VMEM((NX, 8, Q), f32),
            pltpu.VMEM((NX, 8, Q), f32),
            pltpu.VMEM((2, KEYS, Q), f32),
            pltpu.VMEM((3, HD, Q), bf16),
            pltpu.VMEM((3, HD, Q), bf16),
            pltpu.VMEM((3, Q // 128, 128), f32),
            pltpu.VMEM((3, Q // 128, 128), f32),
            pltpu.VMEM((128, HD), bf16),
            pltpu.VMEM((NX, 24, 128), f32),
            pltpu.VMEM((NZ, 1024, 256), bf16),
            pltpu.VMEM((2, 2, ROWS, 512), bf16),
            pltpu.VMEM((17, ROWS, 256), bf16),
            pltpu.VMEM((17, ROWS, 256), bf16),
            dma((5,)),
        ] + [dma((3,))] * 12 + [
            dma((2,)), dma((2,)), dma((4,)), dma((4,)), dma((2,)), dma((2,)),
            dma((NZ,)), dma((NZ,)), dma((3,)), dma((3,)), dma((17,)), dma((17,)),
            dma, dma, dma((6,)), dma((6,)), dma((NZ,)), dma((NZ,)),
        ],
        compiler_params=pltpu.CompilerParams(
            collective_id=0, has_side_effects=True, vmem_limit_bytes=60 * 2 ** 20
        ),
        cost_estimate=pl.CostEstimate(
            flops=4 * NX * Q * NS * KEYS * HD, bytes_accessed=4 * 2 ** 20,
            transcendentals=NX * Q * NS * KEYS,
        ),
        name="attention_and_projection",
    )(q, fresh, prefix, probe, pair, w)


def placement_kernel(
    ids_ref, member_ref, rows_hbm, y_ref, dec_ref, out_ref, y_out, dec_out, sem
):
    me = lax.axis_index("inst")
    size = BLK * 2

    def block(b, n):
        return pltpu.make_async_copy(
            rows_hbm.at[pl.ds(b * size, size)], out_ref.at[pl.ds(n * size, size)], sem.at[n]
        )

    def take(b, taken):
        mine = ids_ref[member_ref[b]] == me

        @pl.when(mine)
        def _():
            block(b, taken).start()

        return taken + mine.astype(jnp.int32)

    taken = lax.fori_loop(0, 32, take, 0)

    def clear(n, carry):
        out_ref[pl.ds(n * size, size), :] = jnp.zeros((size, HD), out_ref.dtype)
        return carry

    lax.fori_loop(taken, CAP, clear, 0)
    y_out[...] = y_ref[...]
    dec_out[...] = dec_ref[...]

    def finish(n, carry):
        block(0, n).wait()
        return carry

    lax.fori_loop(0, taken, finish, 0)


def placement(ids, members, rows, y, dec):
    vmem = pl.BlockSpec(memory_space=pltpu.VMEM)
    return pl.pallas_call(
        placement_kernel,
        out_shape=(
            jax.ShapeDtypeStruct((CAP * BLK * 2, HD), jnp.bfloat16),
            jax.ShapeDtypeStruct(y.shape, y.dtype),
            jax.ShapeDtypeStruct(dec.shape, dec.dtype),
        ),
        in_specs=[pl.BlockSpec(memory_space=pltpu.SMEM)] * 2
        + [pl.BlockSpec(memory_space=pl.ANY), vmem, vmem],
        out_specs=(vmem,) * 3,
        scratch_shapes=[pltpu.SemaphoreType.DMA((CAP,))],
        compiler_params=pltpu.CompilerParams(vmem_limit_bytes=60 * 2 ** 20),
        name="placement",
    )(ids, members, rows, y, dec)


def on_device(
    fresh_segment_probes,
    fresh_segment_pairs,
    earlier_stored_pairs,
    emitted_token_probe,
    emitted_token_pair,
    final_projection_weights,
    remaining_instance_ids,
    segment_destination_member,
):
    span_hidden, decode_attention, moved = fused(
        fresh_segment_probes.reshape(Q, HD),
        fresh_segment_pairs.reshape(ROWS * 2, HD),
        earlier_stored_pairs.reshape(4 * ROWS * 2, HD),
        emitted_token_probe,
        emitted_token_pair.reshape(2, HD),
        final_projection_weights,
    )
    cache, span_hidden, decode_attention = placement(
        remaining_instance_ids, segment_destination_member.reshape(-1),
        moved.reshape(-1, HD), span_hidden, decode_attention,
    )
    return span_hidden, cache.reshape(1, CAP * BLK, 2, 1, HD), decode_attention


def solution(mesh):
    return jax.shard_map(
        on_device,
        mesh=mesh,
        in_specs=(
            P("inst", "tp", None),
            P("inst", None, "tp", None),
            P("inst", None, "tp", None),
            P("tp", None),
            P(None, "tp", None),
            P("tp", "inst"),
            P(),
            P(),
        ),
        out_specs=(P("inst", "tp"), P("inst", None, None, "tp", None), P("tp", None)),
        check_vma=False,
    )
```

```python
import functools
import jax
import jax.numpy as jnp
from jax import lax
from jax.experimental import pallas as pl
from jax.experimental.pallas import tpu as pltpu
from jax.sharding import PartitionSpec as P

BLK = 128
CAP = 8
ROWS = 256
HEADS = 4
HD = 128
Q = ROWS * HEADS
KEYS = 1280
PIECE = 256
NX = 4
NS = 4
NZ = 8
NEG = -1e30
C2 = float(HD ** -0.5 * 1.4426950408889634)
MESH = pl.DeviceIdType.MESH


def signal(where):
    pl.semaphore_signal(
        pltpu.get_barrier_semaphore(), inc=1, device_id=where, device_id_type=MESH
    )


def fused_kernel(
    q_hbm, fresh_hbm, prefix_hbm, probe_ref, pair_ref, w_hbm,
    y_ref, dec_ref, moved,
    raw, raw_q, stage, qbuf, kbuf, vbuf, acc, m_s, l_s, s_buf,
    o_send, o_recv, st_send, st_recv, qd, d_all, w_all, abuf, sbuf, rbuf,
    loc_sem, q_ss, q_rs, k_ss, k_rs, v_ss, v_rs, o_ss, o_rs, t_ss, t_rs, d_ss, d_rs,
    wy_ss, wy_rs, wx_ss, wx_rs, wf_ss, wf_rs, wc_ss, wc_rs, a_ss, a_rs, r_ss, r_rs,
    cy_ss, cy_rs, cx_ss, cx_rs, cc_ss, cc_rs, qf_ss, qf_rs,
):
    me = lax.axis_index("inst")
    tp = lax.axis_index("tp")
    x, s = me // NS, me % NS
    far, core = s // 2, s % 2
    z, low = tp // 2, tp % 2
    s1 = s + 1 - 2 * core
    s2 = (s + 2) % NS
    s3 = (s1 + 2) % NS

    def at_x(d):
        return {"inst": ((x + d) % NX) * NS + s}

    def at_s(t):
        return {"inst": x * NS + t}

    def at_w(t):
        return {"inst": x * NS + 2 * t + low, "tp": z * 2 + core}

    def at_z(d, t):
        return {"inst": x * NS + t, "tp": ((z + d + NZ) % NZ) * 2 + low}

    def at_low(t):
        return {"inst": x * NS + t, "tp": z * 2 + 1 - low}

    def remote(src, dst, ss, rs, where):
        return pltpu.make_async_remote_copy(
            src_ref=src, dst_ref=dst, send_sem=ss, recv_sem=rs,
            device_id=where, device_id_type=MESH,
        )

    load = [
        pltpu.make_async_copy(prefix_hbm, raw.at[0:2048], loc_sem.at[0]),
        pltpu.make_async_copy(fresh_hbm, raw.at[2048:2560], loc_sem.at[1]),
        pltpu.make_async_copy(q_hbm, raw_q, loc_sem.at[2]),
    ]
    for copy in (load[2], load[0], load[1]):
        copy.start()

    for d in (1, 2, 3):
        signal(at_x(d))
    signal(at_s(s1))
    signal(at_s(s2))
    signal(at_low(s))
    signal(at_low(s2))
    for d in (1, -1):
        signal(at_z(d, s))
        signal(at_z(d, s2))

    @pl.when(core != low)
    def _():
        signal(at_w(0))
        signal(at_w(1))

    load[2].wait()
    stage[0:Q] = raw_q[...].astype(jnp.float32)
    for h in range(HEADS):
        qbuf[0, h * ROWS:(h + 1) * ROWS, :] = stage[
            pl.ds(h, ROWS, stride=HEADS), :
        ].astype(jnp.bfloat16)

    pl.semaphore_wait(pltpu.get_barrier_semaphore(), 11 + 2 * ((core + low) % 2))

    def q_push(d):
        return remote(
            qbuf.at[0], qbuf.at[NX - d], q_ss.at[d - 1], q_rs.at[NX - d - 1], at_x(d)
        )

    def q_forward(way):
        part = pl.ds(way * (Q // 2), Q // 2)
        return remote(
            qbuf.at[3 if way == 0 else 1, part], qbuf.at[2, part],
            qf_ss.at[way], qf_rs.at[way], at_x(1 if way == 0 else 3),
        )

    k_push = [
        remote(kbuf.at[s], kbuf.at[s], k_ss.at[0], k_rs.at[0], at_s(s1)),
        remote(kbuf.at[s], kbuf.at[s], k_ss.at[1], k_rs.at[1], at_s(s2)),
        remote(kbuf.at[s2], kbuf.at[s2], k_ss.at[2], k_rs.at[2], at_s(s1)),
    ]
    v_push = [
        remote(vbuf.at[s], vbuf.at[s], v_ss.at[0], v_rs.at[0], at_s(s1)),
        remote(vbuf.at[s], vbuf.at[s], v_ss.at[1], v_rs.at[1], at_s(s2)),
        remote(vbuf.at[s2], vbuf.at[s2], v_ss.at[2], v_rs.at[2], at_s(s1)),
    ]
    half_rows = pl.ds(pl.multiple_of(core * 512, 512), 512)

    def wy_push(t):
        return remote(
            w_hbm.at[:, t * 256:(t + 1) * 256],
            w_all.at[2 * x + far, pl.ds(pl.multiple_of(low * 512, 512), 512)],
            wy_ss.at[t], wy_rs.at[far], at_w(t),
        )

    def wy_keep(t):
        return pltpu.make_async_copy(
            w_hbm.at[:, t * 256:(t + 1) * 256],
            w_all.at[2 * x + far, pl.ds(pl.multiple_of(low * 512, 512), 512)],
            loc_sem.at[3],
        )

    def each_wy(act, keep):
        for t in (0, 1):
            itself = jnp.logical_and(core == low, far == t)

            @pl.when(itself)
            def _():
                keep(t)

            @pl.when(jnp.logical_not(itself))
            def _():
                act(t)

    def wy_arrival(t):
        piece = w_all.at[2 * x + t, half_rows]
        return remote(piece, piece, wy_ss.at[t], wy_rs.at[t], at_w(t))

    def w_piece(chunk):
        return w_all.at[chunk, half_rows]

    def wx_push(way, g):
        n = way * 2 + g
        piece = w_piece(2 * x + g)
        return remote(piece, piece, wx_ss.at[n], wx_rs.at[n], at_x(1 if way == 0 else 3))

    def wf_push(way):
        origin = (x + (3 if way == 0 else 1)) % NX
        piece = w_piece(2 * origin + way)
        return remote(piece, piece, wf_ss.at[way], wf_rs.at[way], at_x(1 if way == 0 else 3))

    def wc_push(chunk):
        piece = w_piece(chunk)
        return remote(piece, piece, wc_ss.at[chunk], wc_rs.at[chunk], at_s(s1))

    def wc_arrival(chunk):
        piece = w_all.at[chunk, pl.ds(pl.multiple_of((1 - core) * 512, 512), 512)]
        return remote(piece, piece, wc_ss.at[chunk], wc_rs.at[chunk], at_s(s1))

    q_push(1).start()
    q_push(3).start()
    load[0].wait()
    load[1].wait()
    stage[...] = raw[...].astype(jnp.float32)
    kbuf[s] = stage[pl.ds(0, KEYS, stride=2), :].astype(jnp.bfloat16)
    k_push[0].start()
    k_push[1].start()
    vbuf[s] = jnp.transpose(stage[pl.ds(1, KEYS, stride=2), :]).astype(jnp.bfloat16)
    v_push[0].start()
    v_push[1].start()

    fresh = raw.at[2048:2560]

    def cy_push():
        return remote(fresh, moved.at[me], cy_ss, cy_rs, at_s(s2))

    def cx_push(n, d):
        src = fresh if n == 0 else moved.at[x * NS + s2]
        dst = moved.at[me] if n == 0 else moved.at[x * NS + s2]
        i = n * 3 + d - 1
        return remote(src, dst, cx_ss.at[i], cx_rs.at[n * 3 + NX - d - 1], at_x(d))

    def cc_push(d, n):
        block = moved.at[((x + d) % NX) * NS + (s, s2)[n]]
        i = d * 2 + n
        return remote(block, block, cc_ss.at[i], cc_rs.at[i], at_s(s1))

    moved_own = pltpu.make_async_copy(fresh, moved.at[me], loc_sem.at[4])

    qd[...] = jnp.zeros_like(qd)
    qd[0:HEADS, :] = probe_ref[...]
    acc[...] = jnp.zeros_like(acc)
    l_s[...] = jnp.zeros_like(l_s)
    m_s[...] = jnp.full(m_s.shape, NEG, jnp.float32)

    key_of = lax.broadcasted_iota(jnp.int32, (PIECE, Q), 0)
    row_of = lax.broadcasted_iota(jnp.int32, (PIECE, Q), 1) % ROWS

    def scores(buf, q, k, j, highest):
        part = lax.dot_general(
            kbuf[k, j * PIECE:(j + 1) * PIECE, :], qbuf[q],
            (((1,), (1,)), ((), ())), preferred_element_type=jnp.float32,
        )
        if j == KEYS // PIECE - 1:
            ahead = ROWS * (((x + q) % NX) * NS + s - (x * NS + k))
            part = jnp.where(key_of - row_of <= ahead, part, NEG)
        s_buf[buf, j * PIECE:(j + 1) * PIECE, :] = part
        return jnp.maximum(highest, jnp.max(part.reshape(PIECE // 8, 8, Q), axis=0))

    lowest = jnp.full((8, Q), NEG, jnp.float32)

    def unit(buf, q, k, highest, following):
        m_old = m_s[q]
        m_new = jnp.maximum(
            m_old, jnp.broadcast_to(jnp.max(highest, axis=0, keepdims=True), (8, Q))
        )
        m_s[q] = m_new
        alpha = jnp.exp2((m_old - m_new) * C2)
        top = m_new[0:1]
        total = acc[q] * alpha[0:1]
        norm = l_s[q] * alpha
        after = lowest
        for j in range(KEYS // PIECE):
            if following is not None:
                after = scores(1 - buf, following[0], following[1], j, after)
            p = jnp.exp2((s_buf[buf, j * PIECE:(j + 1) * PIECE, :] - top) * C2)
            norm = norm + jnp.sum(p.reshape(PIECE // 8, 8, Q), axis=0)
            total = total + jnp.dot(
                vbuf[k, :, j * PIECE:(j + 1) * PIECE], p.astype(jnp.bfloat16),
                preferred_element_type=jnp.float32,
            )
        acc[q] = total
        l_s[q] = norm
        return after

    def q_at(i):
        phase, n = i // 4, i % 4
        near = n + n // 2 - 2 * (n // 3)
        there = 2 - n + 3 * (n // 2) - 2 * (n // 3)
        return near * (1 - phase) + there * phase

    def k_at(i):
        phase = i // 4
        return s * (1 - phase) + s2 * phase, s1 * (1 - phase) + s3 * phase

    def normalised(q, t):
        cols = slice(t * 128, (t + 1) * 128)
        norm = jnp.sum(l_s[q, :, cols], axis=0, keepdims=True)
        return acc[q, :, cols] / norm, m_s[q, 0:1, cols] * C2 + jnp.log2(norm)

    def o_push(d):
        return remote(
            o_send.at[d - 1], o_recv.at[NX - d - 1], o_ss.at[d - 1], o_rs.at[NX - d - 1], at_x(d)
        )

    def t_push(d):
        return remote(
            st_send.at[d - 1], st_recv.at[NX - d - 1], t_ss.at[d - 1], t_rs.at[NX - d - 1], at_x(d)
        )

    highest = lowest
    for j in range(KEYS // PIECE):
        highest = scores(0, 0, s, j, highest)

    def pair(i, highest):
        q = q_at(i)
        ka, kb = k_at(i)

        @pl.when(i == 0)
        def _():
            k_push[0].wait_recv()
            v_push[0].wait_recv()

        @pl.when(i == 4)
        def _():
            k_push[2].wait_recv()
            v_push[2].wait_recv()

        highest = unit(0, q, ka, highest, (q, kb))

        @pl.when(i == 0)
        def _():
            q_push(3).wait_recv()
            q_forward(1).start()
            q_push(1).wait_recv()
            q_forward(0).start()

        @pl.when(i == 2)
        def _():
            q_forward(0).wait_recv()
            q_forward(1).wait_recv()

        @pl.when(i == 3)
        def _():
            k_push[1].wait_recv()
            k_push[2].start()
            v_push[1].wait_recv()
            v_push[2].start()

        highest = unit(1, q, kb, highest, (q_at(i + 1), k_at(i + 1)[0]))

        @pl.when(i == 1)
        def _():
            each_wy(lambda t: wy_push(t).start(), lambda t: wy_keep(t).start())

        @pl.when(i == 3)
        def _():
            each_wy(lambda t: wy_arrival(t).wait_recv(), lambda t: wy_keep(t).wait())
            for g in (0, 1):
                wx_push(0, g).start()
                wx_push(1, g).start()
            wc_push(2 * x).start()
            wc_push(2 * x + 1).start()

        @pl.when(i >= 4)
        def _():
            for t in range(Q // 128):
                o, lse = normalised(q, t)
                o_send[q - 1, :, t * 128:(t + 1) * 128] = o.astype(jnp.bfloat16)
                st_send[q - 1, t:t + 1, :] = lse
            o_push(q).start()
            t_push(q).start()

        @pl.when(i == 4)
        def _():
            cy_push().start()
            moved_own.start()

        @pl.when(i == 6)
        def _():
            for way in (0, 1):
                origin = (x + (3 if way == 0 else 1)) % NX
                wx_push(way, way).wait_recv()
                wf_push(way).start()
                wx_push(way, 1 - way).wait_recv()
                wc_push(2 * origin).start()
                wc_push(2 * origin + 1).start()

        return highest

    highest = lax.fori_loop(0, 7, pair, highest)
    highest = unit(0, 0, s2, highest, (0, s3))
    unit(1, 0, s3, highest, None)

    dm = jnp.full((1, 128), NEG, jnp.float32)
    dl = jnp.zeros((1, 128), jnp.float32)
    da = jnp.zeros((HD, 128), jnp.float32)
    for k in range(NS):
        part = lax.dot_general(
            kbuf[k], qd[...], (((1,), (1,)), ((), ())), preferred_element_type=jnp.float32
        )
        new = jnp.maximum(dm, jnp.max(part, axis=0, keepdims=True))
        alpha = jnp.exp2((dm - new) * C2)
        p = jnp.exp2((part - new) * C2)
        dl = dl * alpha + jnp.sum(p, axis=0, keepdims=True)
        da = da * alpha + jnp.dot(
            vbuf[k], p.astype(jnp.bfloat16), preferred_element_type=jnp.float32
        )
        dm = new
    d_all[x, 0:8, :] = jnp.transpose(da)[0:8]
    d_all[x, 8:16, :] = jnp.transpose(jnp.broadcast_to(dm, (128, 128)))[0:8]
    d_all[x, 16:24, :] = jnp.transpose(jnp.broadcast_to(dl, (128, 128)))[0:8]

    def d_push(d):
        return remote(d_all.at[x], d_all.at[x], d_ss.at[d - 1], d_rs.at[NX - d - 1], at_x(d))

    for d in (1, 2, 3):
        d_push(d).start()

    for d in (1, 2, 3):
        o_push(d).wait_recv()
        t_push(d).wait_recv()
    for t in range(Q // 128):
        cols = slice(t * 128, (t + 1) * 128)
        o, lse = normalised(0, t)
        rest = [st_recv[d, t:t + 1, :] for d in range(3)]
        top = functools.reduce(jnp.maximum, rest, lse)
        weight = jnp.exp2(lse - top)
        total, norm = o * weight, weight
        for d in range(3):
            weight = jnp.exp2(rest[d] - top)
            total = total + o_recv[d, :, cols].astype(jnp.float32) * weight
            norm = norm + weight
        h, r = t // 2, (t % 2) * 128
        abuf[0, low, r:r + 128, h * HD:(h + 1) * HD] = jnp.transpose(total / norm).astype(
            jnp.bfloat16
        )

    a_push = [
        remote(abuf.at[0, low], abuf.at[0, low], a_ss.at[0], a_rs.at[0], at_low(s)),
        remote(abuf.at[0, low], abuf.at[1, low], a_ss.at[1], a_rs.at[1], at_low(s2)),
        remote(abuf.at[0, low], abuf.at[1, low], a_ss.at[2], a_rs.at[2], at_s(s2)),
    ]
    for copy in a_push:
        copy.start()
    for d in (1, 2, 3):
        d_push(d).wait_recv()
    query = qd[0:8, :].astype(jnp.float32)
    last = jnp.sum(query * pair_ref[0:1, :].astype(jnp.float32), axis=1, keepdims=True)
    last = jnp.broadcast_to(last, (8, HD))
    top = last
    for d in range(NX):
        top = jnp.maximum(top, d_all[d, 8:16, :])
    weight = jnp.exp2((last - top) * C2)
    total, norm = weight * pair_ref[1:2, :].astype(jnp.float32), weight
    for d in range(NX):
        weight = jnp.exp2((d_all[d, 8:16, :] - top) * C2)
        total = total + d_all[d, 0:8, :] * weight
        norm = norm + d_all[d, 16:24, :] * weight
    dec_ref[...] = (total / norm)[0:HEADS].astype(jnp.bfloat16)

    for way in (0, 1):
        wf_push(way).wait_recv()
        wc_push(2 * ((x + 2) % NX) + way).start()
    cy_push().wait_recv()
    moved_own.wait()
    for n in (0, 1):
        for d in (1, 3, 2):
            cx_push(n, d).start()
        cc_push(0, n).start()

    present = set()

    def term(d, r):
        chunk = (z + d + NZ) % NZ
        if d not in present:
            present.add(d)
            wc_arrival(chunk).wait_recv()
        return jnp.dot(
            abuf[r, 0], w_all[chunk, 0:512, :], preferred_element_type=jnp.float32
        ) + jnp.dot(abuf[r, 1], w_all[chunk, 512:1024, :], preferred_element_type=jnp.float32)

    def push(way, step, r, p):
        n = (way * 4 + step) * 4 + r * 2 + p
        return remote(
            sbuf.at[n], rbuf.at[n], r_ss.at[n], r_rs.at[n],
            at_z(1 if way == 0 else -1, s2 if (step == 3 and r == 1) else s),
        )

    sent = []

    def send(way, step, r, value, add):
        for p in (0, 1):
            part = value[p * 128:(p + 1) * 128]
            if add:
                part = part + arrived(way, step - 1, r, p)
            sbuf[(way * 4 + step) * 4 + r * 2 + p] = part.astype(jnp.bfloat16)
            copy = push(way, step, r, p)
            copy.start()
            sent.append(copy)

    def arrived(way, step, r, p):
        push(way, step, r, p).wait_recv()
        return rbuf[(way * 4 + step) * 4 + r * 2 + p].astype(jnp.float32)

    a_push[0].wait_recv()
    send(0, 0, 0, term(4, 0), False)
    send(1, 1, 0, term(-3, 0), False)
    a_push[1].wait_recv()
    a_push[2].wait_recv()
    send(1, 0, 1, term(4, 1), False)
    send(0, 1, 1, term(3, 1), False)
    send(0, 1, 0, term(3, 0), True)
    send(1, 1, 1, term(-3, 1), True)
    last_term = term(0, 1)
    others = []
    for p in (0, 1):
        n = 32 + p
        sbuf[n] = last_term[p * 128:(p + 1) * 128].astype(jnp.bfloat16)
        others.append(remote(sbuf.at[n], rbuf.at[n], r_ss.at[n], r_rs.at[n], at_s(s2)))
        others[p].start()
    for step in (2, 3):
        send(1, step, 0, term(step - 4, 0), True)
        send(0, step, 1, term(4 - step, 1), True)
        send(0, step, 0, term(4 - step, 0), True)
        send(1, step, 1, term(step - 4, 1), True)
    for d in (1, 3, 2):
        for n in (0, 1):
            cx_push(n, NX - d).wait_recv()
            cc_push(d, n).start()
    last_term = term(0, 0)
    for p in (0, 1):
        rows = slice(p * 128, (p + 1) * 128)
        total = last_term[rows] + arrived(1, 3, 0, p) + arrived(0, 3, 0, p)
        y_ref[rows, pl.ds(pl.multiple_of(far * 256, 256), 256)] = total.astype(jnp.bfloat16)
    for p in (0, 1):
        rows = slice(p * 128, (p + 1) * 128)
        others[p].wait_recv()
        total = rbuf[32 + p].astype(jnp.float32) + arrived(0, 3, 1, p) + arrived(1, 3, 1, p)
        y_ref[rows, pl.ds(pl.multiple_of((1 - far) * 256, 256), 256)] = total.astype(jnp.bfloat16)

    cy_push().wait_send()
    for n in (0, 1):
        for d in (1, 2, 3):
            cx_push(n, d).wait_send()
        for d in range(NX):
            cc_push(d, n).wait_send()
            cc_push(d, n).wait_recv()
    for copy in sent + others + a_push + k_push + v_push:
        copy.wait_send()
    for d in (1, 2, 3):
        o_push(d).wait_send()
        t_push(d).wait_send()
        d_push(d).wait_send()
    q_push(1).wait_send()
    q_push(3).wait_send()
    q_forward(0).wait_send()
    q_forward(1).wait_send()
    each_wy(lambda t: wy_push(t).wait_send(), lambda t: None)
    for way in (0, 1):
        wx_push(way, 0).wait_send()
        wx_push(way, 1).wait_send()
        wf_push(way).wait_send()
    for chunk in range(NZ):
        wc_push(chunk).wait_send()


def fused(q, fresh, prefix, probe, pair, w):
    dma = pltpu.SemaphoreType.DMA
    bf16, f32 = jnp.bfloat16, jnp.float32
    return pl.pallas_call(
        fused_kernel,
        out_shape=(
            jax.ShapeDtypeStruct((ROWS, 512), bf16),
            jax.ShapeDtypeStruct((HEADS, HD), bf16),
            jax.ShapeDtypeStruct((NX * NS, 2 * ROWS, HD), bf16),
        ),
        in_specs=[pl.BlockSpec(memory_space=pl.ANY)] * 3
        + [pl.BlockSpec(memory_space=pltpu.VMEM)] * 2
        + [pl.BlockSpec(memory_space=pl.ANY)],
        out_specs=(pl.BlockSpec(memory_space=pltpu.VMEM),) * 2
        + (pl.BlockSpec(memory_space=pl.ANY),),
        scratch_shapes=[
            pltpu.VMEM((2 * KEYS, HD), bf16),
            pltpu.VMEM((Q, HD), bf16),
            pltpu.VMEM((2 * KEYS, HD), f32),
            pltpu.VMEM((NX, Q, HD), bf16),
            pltpu.VMEM((NS, KEYS, HD), bf16),
            pltpu.VMEM((NS, HD, KEYS), bf16),
            pltpu.VMEM((NX, HD, Q), f32),
            pltpu.VMEM((NX, 8, Q), f32),
            pltpu.VMEM((NX, 8, Q), f32),
            pltpu.VMEM((2, KEYS, Q), f32),
            pltpu.VMEM((3, HD, Q), bf16),
            pltpu.VMEM((3, HD, Q), bf16),
            pltpu.VMEM((3, Q // 128, 128), f32),
            pltpu.VMEM((3, Q // 128, 128), f32),
            pltpu.VMEM((128, HD), bf16),
            pltpu.VMEM((NX, 24, 128), f32),
            pltpu.VMEM((NZ, 1024, 256), bf16),
            pltpu.VMEM((2, 2, ROWS, 512), bf16),
            pltpu.VMEM((34, 128, 256), bf16),
            pltpu.VMEM((34, 128, 256), bf16),
            dma((5,)),
        ] + [dma((3,))] * 12 + [
            dma((2,)), dma((2,)), dma((4,)), dma((4,)), dma((2,)), dma((2,)),
            dma((NZ,)), dma((NZ,)), dma((3,)), dma((3,)), dma((34,)), dma((34,)),
            dma, dma, dma((6,)), dma((6,)), dma((NZ,)), dma((NZ,)), dma((2,)), dma((2,)),
        ],
        compiler_params=pltpu.CompilerParams(
            collective_id=0, has_side_effects=True, vmem_limit_bytes=60 * 2 ** 20
        ),
        cost_estimate=pl.CostEstimate(
            flops=4 * NX * Q * NS * KEYS * HD, bytes_accessed=4 * 2 ** 20,
            transcendentals=NX * Q * NS * KEYS,
        ),
        name="attention_and_projection",
    )(q, fresh, prefix, probe, pair, w)


def placement_kernel(
    ids_ref, member_ref, rows_hbm, y_ref, dec_ref, out_ref, y_out, dec_out, sem
):
    me = lax.axis_index("inst")
    size = BLK * 2

    def block(b, n):
        return pltpu.make_async_copy(
            rows_hbm.at[pl.ds(b * size, size)], out_ref.at[pl.ds(n * size, size)], sem.at[n]
        )

    def take(b, taken):
        mine = ids_ref[member_ref[b]] == me

        @pl.when(mine)
        def _():
            block(b, taken).start()

        return taken + mine.astype(jnp.int32)

    taken = lax.fori_loop(0, 32, take, 0)

    def clear(n, carry):
        out_ref[pl.ds(n * size, size), :] = jnp.zeros((size, HD), out_ref.dtype)
        return carry

    lax.fori_loop(taken, CAP, clear, 0)
    y_out[...] = y_ref[...]
    dec_out[...] = dec_ref[...]

    def finish(n, carry):
        block(0, n).wait()
        return carry

    lax.fori_loop(0, taken, finish, 0)


def placement(ids, members, rows, y, dec):
    vmem = pl.BlockSpec(memory_space=pltpu.VMEM)
    return pl.pallas_call(
        placement_kernel,
        out_shape=(
            jax.ShapeDtypeStruct((CAP * BLK * 2, HD), jnp.bfloat16),
            jax.ShapeDtypeStruct(y.shape, y.dtype),
            jax.ShapeDtypeStruct(dec.shape, dec.dtype),
        ),
        in_specs=[pl.BlockSpec(memory_space=pltpu.SMEM)] * 2
        + [pl.BlockSpec(memory_space=pl.ANY), vmem, vmem],
        out_specs=(vmem,) * 3,
        scratch_shapes=[pltpu.SemaphoreType.DMA((CAP,))],
        compiler_params=pltpu.CompilerParams(vmem_limit_bytes=60 * 2 ** 20),
        name="placement",
    )(ids, members, rows, y, dec)


def on_device(
    fresh_segment_probes,
    fresh_segment_pairs,
    earlier_stored_pairs,
    emitted_token_probe,
    emitted_token_pair,
    final_projection_weights,
    remaining_instance_ids,
    segment_destination_member,
):
    span_hidden, decode_attention, moved = fused(
        fresh_segment_probes.reshape(Q, HD),
        fresh_segment_pairs.reshape(ROWS * 2, HD),
        earlier_stored_pairs.reshape(4 * ROWS * 2, HD),
        emitted_token_probe,
        emitted_token_pair.reshape(2, HD),
        final_projection_weights,
    )
    cache, span_hidden, decode_attention = placement(
        remaining_instance_ids, segment_destination_member.reshape(-1),
        moved.reshape(-1, HD), span_hidden, decode_attention,
    )
    return span_hidden, cache.reshape(1, CAP * BLK, 2, 1, HD), decode_attention


def solution(mesh):
    return jax.shard_map(
        on_device,
        mesh=mesh,
        in_specs=(
            P("inst", "tp", None),
            P("inst", None, "tp", None),
            P("inst", None, "tp", None),
            P("tp", None),
            P(None, "tp", None),
            P("tp", "inst"),
            P(),
            P(),
        ),
        out_specs=(P("inst", "tp"), P("inst", None, None, "tp", None), P("tp", None)),
        check_vma=False,
    )
```

```python
import functools
import jax
import jax.numpy as jnp
from jax import lax
from jax.experimental import pallas as pl
from jax.experimental.pallas import tpu as pltpu
from jax.sharding import PartitionSpec as P

BLK = 128
CAP = 8
ROWS = 256
HEADS = 4
HD = 128
Q = ROWS * HEADS
KEYS = 1280
PIECE = 256
NX = 4
NS = 4
NZ = 8
NEG = -1e30
C2 = float(HD ** -0.5 * 1.4426950408889634)
MESH = pl.DeviceIdType.MESH


def signal(where):
    pl.semaphore_signal(
        pltpu.get_barrier_semaphore(), inc=1, device_id=where, device_id_type=MESH
    )


def fused_kernel(
    q_hbm, fresh_hbm, prefix_hbm, probe_ref, pair_ref, w_hbm,
    y_ref, dec_ref, moved,
    raw, raw_q, stage, qbuf, kbuf, vbuf, acc, m_s, l_s, s_buf,
    o_send, o_recv, st_send, st_recv, qd, d_all, w_all, abuf, sbuf, rbuf,
    loc_sem, q_ss, q_rs, k_ss, k_rs, v_ss, v_rs, o_ss, o_rs, t_ss, t_rs, d_ss, d_rs,
    wy_ss, wy_rs, wx_ss, wx_rs, wf_ss, wf_rs, wc_ss, wc_rs, a_ss, a_rs, r_ss, r_rs,
    cy_ss, cy_rs, cx_ss, cx_rs, cc_ss, cc_rs, qf_ss, qf_rs,
):
    me = lax.axis_index("inst")
    tp = lax.axis_index("tp")
    x, s = me // NS, me % NS
    far, core = s // 2, s % 2
    z, low = tp // 2, tp % 2
    s1 = s + 1 - 2 * core
    s2 = (s + 2) % NS
    s3 = (s1 + 2) % NS

    def at_x(d):
        return {"inst": ((x + d) % NX) * NS + s}

    def at_s(t):
        return {"inst": x * NS + t}

    def at_w(t):
        return {"inst": x * NS + 2 * t + low, "tp": z * 2 + core}

    def at_z(d, t):
        return {"inst": x * NS + t, "tp": ((z + d + NZ) % NZ) * 2 + low}

    def at_low(t):
        return {"inst": x * NS + t, "tp": z * 2 + 1 - low}

    def remote(src, dst, ss, rs, where):
        return pltpu.make_async_remote_copy(
            src_ref=src, dst_ref=dst, send_sem=ss, recv_sem=rs,
            device_id=where, device_id_type=MESH,
        )

    load = [
        pltpu.make_async_copy(prefix_hbm, raw.at[0:2048], loc_sem.at[0]),
        pltpu.make_async_copy(fresh_hbm, raw.at[2048:2560], loc_sem.at[1]),
        pltpu.make_async_copy(q_hbm, raw_q, loc_sem.at[2]),
    ]
    for copy in (load[2], load[0], load[1]):
        copy.start()

    for d in (1, 2, 3):
        signal(at_x(d))
    signal(at_s(s1))
    signal(at_s(s2))
    signal(at_low(s))
    signal(at_low(s2))
    for d in (1, -1):
        signal(at_z(d, s))
        signal(at_z(d, s2))

    @pl.when(core != low)
    def _():
        signal(at_w(0))
        signal(at_w(1))

    load[2].wait()
    stage[0:Q] = raw_q[...].astype(jnp.float32)
    for h in range(HEADS):
        qbuf[0, h * ROWS:(h + 1) * ROWS, :] = stage[
            pl.ds(h, ROWS, stride=HEADS), :
        ].astype(jnp.bfloat16)

    pl.semaphore_wait(pltpu.get_barrier_semaphore(), 11 + 2 * ((core + low) % 2))

    def q_push(d):
        return remote(
            qbuf.at[0], qbuf.at[NX - d], q_ss.at[d - 1], q_rs.at[NX - d - 1], at_x(d)
        )

    def q_forward(way):
        part = pl.ds(way * (Q // 2), Q // 2)
        return remote(
            qbuf.at[3 if way == 0 else 1, part], qbuf.at[2, part],
            qf_ss.at[way], qf_rs.at[way], at_x(1 if way == 0 else 3),
        )

    k_push = [
        remote(kbuf.at[s], kbuf.at[s], k_ss.at[0], k_rs.at[0], at_s(s1)),
        remote(kbuf.at[s], kbuf.at[s], k_ss.at[1], k_rs.at[1], at_s(s2)),
        remote(kbuf.at[s2], kbuf.at[s2], k_ss.at[2], k_rs.at[2], at_s(s1)),
    ]
    v_push = [
        remote(vbuf.at[s], vbuf.at[s], v_ss.at[0], v_rs.at[0], at_s(s1)),
        remote(vbuf.at[s], vbuf.at[s], v_ss.at[1], v_rs.at[1], at_s(s2)),
        remote(vbuf.at[s2], vbuf.at[s2], v_ss.at[2], v_rs.at[2], at_s(s1)),
    ]
    half_rows = pl.ds(pl.multiple_of(core * 512, 512), 512)

    def wy_push(t):
        return remote(
            w_hbm.at[:, t * 256:(t + 1) * 256],
            w_all.at[2 * x + far, pl.ds(pl.multiple_of(low * 512, 512), 512)],
            wy_ss.at[t], wy_rs.at[far], at_w(t),
        )

    def wy_keep(t):
        return pltpu.make_async_copy(
            w_hbm.at[:, t * 256:(t + 1) * 256],
            w_all.at[2 * x + far, pl.ds(pl.multiple_of(low * 512, 512), 512)],
            loc_sem.at[3],
        )

    def each_wy(act, keep):
        for t in (0, 1):
            itself = jnp.logical_and(core == low, far == t)

            @pl.when(itself)
            def _():
                keep(t)

            @pl.when(jnp.logical_not(itself))
            def _():
                act(t)

    def wy_arrival(t):
        piece = w_all.at[2 * x + t, half_rows]
        return remote(piece, piece, wy_ss.at[t], wy_rs.at[t], at_w(t))

    def w_piece(chunk):
        return w_all.at[chunk, half_rows]

    def wx_push(way, g):
        n = way * 2 + g
        piece = w_piece(2 * x + g)
        return remote(piece, piece, wx_ss.at[n], wx_rs.at[n], at_x(1 if way == 0 else 3))

    def wf_push(way):
        origin = (x + (3 if way == 0 else 1)) % NX
        piece = w_piece(2 * origin + way)
        return remote(piece, piece, wf_ss.at[way], wf_rs.at[way], at_x(1 if way == 0 else 3))

    def wc_push(chunk):
        piece = w_piece(chunk)
        return remote(piece, piece, wc_ss.at[chunk], wc_rs.at[chunk], at_s(s1))

    def wc_arrival(chunk):
        piece = w_all.at[chunk, pl.ds(pl.multiple_of((1 - core) * 512, 512), 512)]
        return remote(piece, piece, wc_ss.at[chunk], wc_rs.at[chunk], at_s(s1))

    q_push(1).start()
    q_push(3).start()
    load[0].wait()
    load[1].wait()
    stage[...] = raw[...].astype(jnp.float32)
    kbuf[s] = stage[pl.ds(0, KEYS, stride=2), :].astype(jnp.bfloat16)
    k_push[0].start()
    k_push[1].start()
    vbuf[s] = jnp.transpose(stage[pl.ds(1, KEYS, stride=2), :]).astype(jnp.bfloat16)
    v_push[0].start()
    v_push[1].start()

    fresh = raw.at[2048:2560]

    def cy_push():
        return remote(fresh, moved.at[me], cy_ss, cy_rs, at_s(s2))

    def cx_push(n, d):
        src = fresh if n == 0 else moved.at[x * NS + s2]
        dst = moved.at[me] if n == 0 else moved.at[x * NS + s2]
        i = n * 3 + d - 1
        return remote(src, dst, cx_ss.at[i], cx_rs.at[n * 3 + NX - d - 1], at_x(d))

    def cc_push(d, n):
        block = moved.at[((x + d) % NX) * NS + (s, s2)[n]]
        i = d * 2 + n
        return remote(block, block, cc_ss.at[i], cc_rs.at[i], at_s(s1))

    moved_own = pltpu.make_async_copy(fresh, moved.at[me], loc_sem.at[4])

    qd[...] = jnp.zeros_like(qd)
    qd[0:HEADS, :] = probe_ref[...]
    acc[...] = jnp.zeros_like(acc)
    l_s[...] = jnp.zeros_like(l_s)
    m_s[...] = jnp.full(m_s.shape, NEG, jnp.float32)

    key_of = lax.broadcasted_iota(jnp.int32, (PIECE, Q), 0)
    row_of = lax.broadcasted_iota(jnp.int32, (PIECE, Q), 1) % ROWS

    def scores(buf, q, k, j, highest):
        part = lax.dot_general(
            kbuf[k, j * PIECE:(j + 1) * PIECE, :], qbuf[q],
            (((1,), (1,)), ((), ())), preferred_element_type=jnp.float32,
        )
        if j == KEYS // PIECE - 1:
            ahead = ROWS * (((x + q) % NX) * NS + s - (x * NS + k))
            part = jnp.where(key_of - row_of <= ahead, part, NEG)
        s_buf[buf, j * PIECE:(j + 1) * PIECE, :] = part
        return jnp.maximum(highest, jnp.max(part.reshape(PIECE // 8, 8, Q), axis=0))

    lowest = jnp.full((8, Q), NEG, jnp.float32)

    def unit(buf, q, k, highest, following):
        m_old = m_s[q]
        m_new = jnp.maximum(
            m_old, jnp.broadcast_to(jnp.max(highest, axis=0, keepdims=True), (8, Q))
        )
        m_s[q] = m_new
        alpha = jnp.exp2((m_old - m_new) * C2)
        top = m_new[0:1]
        total = acc[q] * alpha[0:1]
        norm = l_s[q] * alpha
        after = lowest
        for j in range(KEYS // PIECE):
            if following is not None:
                after = scores(1 - buf, following[0], following[1], j, after)
            p = jnp.exp2((s_buf[buf, j * PIECE:(j + 1) * PIECE, :] - top) * C2)
            norm = norm + jnp.sum(p.reshape(PIECE // 8, 8, Q), axis=0)
            total = total + jnp.dot(
                vbuf[k, :, j * PIECE:(j + 1) * PIECE], p.astype(jnp.bfloat16),
                preferred_element_type=jnp.float32,
            )
        acc[q] = total
        l_s[q] = norm
        return after

    def q_at(i):
        phase, n = i // 4, i % 4
        near = n + n // 2 - 2 * (n // 3)
        there = 2 - n + 3 * (n // 2) - 2 * (n // 3)
        return near * (1 - phase) + there * phase

    def k_at(i):
        phase = i // 4
        return s * (1 - phase) + s2 * phase, s1 * (1 - phase) + s3 * phase

    def normalised(q, t):
        cols = slice(t * 128, (t + 1) * 128)
        norm = jnp.sum(l_s[q, :, cols], axis=0, keepdims=True)
        return acc[q, :, cols] / norm, m_s[q, 0:1, cols] * C2 + jnp.log2(norm)

    def o_push(d):
        return remote(
            o_send.at[d - 1], o_recv.at[NX - d - 1], o_ss.at[d - 1], o_rs.at[NX - d - 1], at_x(d)
        )

    def t_push(d):
        return remote(
            st_send.at[d - 1], st_recv.at[NX - d - 1], t_ss.at[d - 1], t_rs.at[NX - d - 1], at_x(d)
        )

    highest = lowest
    for j in range(KEYS // PIECE):
        highest = scores(0, 0, s, j, highest)

    def pair(i, highest):
        q = q_at(i)
        ka, kb = k_at(i)

        @pl.when(i == 4)
        def _():
            k_push[2].wait_recv()
            v_push[2].wait_recv()

        highest = unit(0, q, ka, highest, (q, kb))

        @pl.when(i == 2)
        def _():
            q_forward(0).wait_recv()
            q_forward(1).wait_recv()

        @pl.when(i == 3)
        def _():
            k_push[1].wait_recv()
            k_push[2].start()
            v_push[1].wait_recv()
            v_push[2].start()

        highest = unit(1, q, kb, highest, (q_at(i + 1), k_at(i + 1)[0]))

        @pl.when(i == 1)
        def _():
            each_wy(lambda t: wy_push(t).start(), lambda t: wy_keep(t).start())

        @pl.when(i == 3)
        def _():
            each_wy(lambda t: wy_arrival(t).wait_recv(), lambda t: wy_keep(t).wait())
            for g in (0, 1):
                wx_push(0, g).start()
                wx_push(1, g).start()
            wc_push(2 * x).start()
            wc_push(2 * x + 1).start()

        @pl.when(i >= 4)
        def _():
            for t in range(Q // 128):
                o, lse = normalised(q, t)
                o_send[q - 1, :, t * 128:(t + 1) * 128] = o.astype(jnp.bfloat16)
                st_send[q - 1, t:t + 1, :] = lse
            o_push(q).start()
            t_push(q).start()

        @pl.when(i == 4)
        def _():
            cy_push().start()
            moved_own.start()

        @pl.when(i == 6)
        def _():
            for way in (0, 1):
                origin = (x + (3 if way == 0 else 1)) % NX
                wx_push(way, way).wait_recv()
                wf_push(way).start()
                wx_push(way, 1 - way).wait_recv()
                wc_push(2 * origin).start()
                wc_push(2 * origin + 1).start()

        return highest

    k_push[0].wait_recv()
    v_push[0].wait_recv()
    highest = unit(0, 0, s, highest, (0, s1))
    unit(1, 0, s1, highest, None)
    q_push(3).wait_recv()
    q_forward(1).start()
    q_push(1).wait_recv()
    q_forward(0).start()
    highest = lowest
    for j in range(KEYS // PIECE):
        highest = scores(0, 1, s, j, highest)
    highest = lax.fori_loop(1, 7, pair, highest)
    highest = unit(0, 0, s2, highest, (0, s3))
    unit(1, 0, s3, highest, None)

    dm = jnp.full((1, 128), NEG, jnp.float32)
    dl = jnp.zeros((1, 128), jnp.float32)
    da = jnp.zeros((HD, 128), jnp.float32)
    for k in range(NS):
        part = lax.dot_general(
            kbuf[k], qd[...], (((1,), (1,)), ((), ())), preferred_element_type=jnp.float32
        )
        new = jnp.maximum(dm, jnp.max(part, axis=0, keepdims=True))
        alpha = jnp.exp2((dm - new) * C2)
        p = jnp.exp2((part - new) * C2)
        dl = dl * alpha + jnp.sum(p, axis=0, keepdims=True)
        da = da * alpha + jnp.dot(
            vbuf[k], p.astype(jnp.bfloat16), preferred_element_type=jnp.float32
        )
        dm = new
    d_all[x, 0:8, :] = jnp.transpose(da)[0:8]
    d_all[x, 8:16, :] = jnp.transpose(jnp.broadcast_to(dm, (128, 128)))[0:8]
    d_all[x, 16:24, :] = jnp.transpose(jnp.broadcast_to(dl, (128, 128)))[0:8]

    def d_push(d):
        return remote(d_all.at[x], d_all.at[x], d_ss.at[d - 1], d_rs.at[NX - d - 1], at_x(d))

    for d in (1, 2, 3):
        d_push(d).start()

    for d in (1, 2, 3):
        o_push(d).wait_recv()
        t_push(d).wait_recv()
    for t in range(Q // 128):
        cols = slice(t * 128, (t + 1) * 128)
        o, lse = normalised(0, t)
        rest = [st_recv[d, t:t + 1, :] for d in range(3)]
        top = functools.reduce(jnp.maximum, rest, lse)
        weight = jnp.exp2(lse - top)
        total, norm = o * weight, weight
        for d in range(3):
            weight = jnp.exp2(rest[d] - top)
            total = total + o_recv[d, :, cols].astype(jnp.float32) * weight
            norm = norm + weight
        h, r = t // 2, (t % 2) * 128
        abuf[0, low, r:r + 128, h * HD:(h + 1) * HD] = jnp.transpose(total / norm).astype(
            jnp.bfloat16
        )

    a_push = [
        remote(abuf.at[0, low], abuf.at[0, low], a_ss.at[0], a_rs.at[0], at_low(s)),
        remote(abuf.at[0, low], abuf.at[1, low], a_ss.at[1], a_rs.at[1], at_low(s2)),
        remote(abuf.at[0, low], abuf.at[1, low], a_ss.at[2], a_rs.at[2], at_s(s2)),
    ]
    for copy in a_push:
        copy.start()
    for d in (1, 2, 3):
        d_push(d).wait_recv()
    query = qd[0:8, :].astype(jnp.float32)
    last = jnp.sum(query * pair_ref[0:1, :].astype(jnp.float32), axis=1, keepdims=True)
    last = jnp.broadcast_to(last, (8, HD))
    top = last
    for d in range(NX):
        top = jnp.maximum(top, d_all[d, 8:16, :])
    weight = jnp.exp2((last - top) * C2)
    total, norm = weight * pair_ref[1:2, :].astype(jnp.float32), weight
    for d in range(NX):
        weight = jnp.exp2((d_all[d, 8:16, :] - top) * C2)
        total = total + d_all[d, 0:8, :] * weight
        norm = norm + d_all[d, 16:24, :] * weight
    dec_ref[...] = (total / norm)[0:HEADS].astype(jnp.bfloat16)

    for way in (0, 1):
        wf_push(way).wait_recv()
        wc_push(2 * ((x + 2) % NX) + way).start()
    cy_push().wait_recv()
    moved_own.wait()
    for n in (0, 1):
        for d in (1, 3, 2):
            cx_push(n, d).start()
        cc_push(0, n).start()

    present = set()

    def term(d, r):
        chunk = (z + d + NZ) % NZ
        if d not in present:
            present.add(d)
            wc_arrival(chunk).wait_recv()
        return jnp.dot(
            abuf[r, 0], w_all[chunk, 0:512, :], preferred_element_type=jnp.float32
        ) + jnp.dot(abuf[r, 1], w_all[chunk, 512:1024, :], preferred_element_type=jnp.float32)

    def push(way, step, r, p):
        n = (way * 4 + step) * 4 + r * 2 + p
        return remote(
            sbuf.at[n], rbuf.at[n], r_ss.at[n], r_rs.at[n],
            at_z(1 if way == 0 else -1, s2 if (step == 3 and r == 1) else s),
        )

    sent = []

    def send(way, step, r, value, add):
        for p in (0, 1):
            part = value[p * 128:(p + 1) * 128]
            if add:
                part = part + arrived(way, step - 1, r, p)
            sbuf[(way * 4 + step) * 4 + r * 2 + p] = part.astype(jnp.bfloat16)
            copy = push(way, step, r, p)
            copy.start()
            sent.append(copy)

    def arrived(way, step, r, p):
        push(way, step, r, p).wait_recv()
        return rbuf[(way * 4 + step) * 4 + r * 2 + p].astype(jnp.float32)

    a_push[0].wait_recv()
    send(0, 0, 0, term(4, 0), False)
    send(1, 1, 0, term(-3, 0), False)
    a_push[1].wait_recv()
    a_push[2].wait_recv()
    send(1, 0, 1, term(4, 1), False)
    send(0, 1, 1, term(3, 1), False)
    send(0, 1, 0, term(3, 0), True)
    send(1, 1, 1, term(-3, 1), True)
    last_term = term(0, 1)
    others = []
    for p in (0, 1):
        n = 32 + p
        sbuf[n] = last_term[p * 128:(p + 1) * 128].astype(jnp.bfloat16)
        others.append(remote(sbuf.at[n], rbuf.at[n], r_ss.at[n], r_rs.at[n], at_s(s2)))
        others[p].start()
    for step in (2, 3):
        send(1, step, 0, term(step - 4, 0), True)
        send(0, step, 1, term(4 - step, 1), True)
        send(0, step, 0, term(4 - step, 0), True)
        send(1, step, 1, term(step - 4, 1), True)
    for d in (1, 3, 2):
        for n in (0, 1):
            cx_push(n, NX - d).wait_recv()
            cc_push(d, n).start()
    last_term = term(0, 0)
    for p in (0, 1):
        rows = slice(p * 128, (p + 1) * 128)
        total = last_term[rows] + arrived(1, 3, 0, p) + arrived(0, 3, 0, p)
        y_ref[rows, pl.ds(pl.multiple_of(far * 256, 256), 256)] = total.astype(jnp.bfloat16)
    for p in (0, 1):
        rows = slice(p * 128, (p + 1) * 128)
        others[p].wait_recv()
        total = rbuf[32 + p].astype(jnp.float32) + arrived(0, 3, 1, p) + arrived(1, 3, 1, p)
        y_ref[rows, pl.ds(pl.multiple_of((1 - far) * 256, 256), 256)] = total.astype(jnp.bfloat16)

    cy_push().wait_send()
    for n in (0, 1):
        for d in (1, 2, 3):
            cx_push(n, d).wait_send()
        for d in range(NX):
            cc_push(d, n).wait_send()
            cc_push(d, n).wait_recv()
    for copy in sent + others + a_push + k_push + v_push:
        copy.wait_send()
    for d in (1, 2, 3):
        o_push(d).wait_send()
        t_push(d).wait_send()
        d_push(d).wait_send()
    q_push(1).wait_send()
    q_push(3).wait_send()
    q_forward(0).wait_send()
    q_forward(1).wait_send()
    each_wy(lambda t: wy_push(t).wait_send(), lambda t: None)
    for way in (0, 1):
        wx_push(way, 0).wait_send()
        wx_push(way, 1).wait_send()
        wf_push(way).wait_send()
    for chunk in range(NZ):
        wc_push(chunk).wait_send()


def fused(q, fresh, prefix, probe, pair, w):
    dma = pltpu.SemaphoreType.DMA
    bf16, f32 = jnp.bfloat16, jnp.float32
    return pl.pallas_call(
        fused_kernel,
        out_shape=(
            jax.ShapeDtypeStruct((ROWS, 512), bf16),
            jax.ShapeDtypeStruct((HEADS, HD), bf16),
            jax.ShapeDtypeStruct((NX * NS, 2 * ROWS, HD), bf16),
        ),
        in_specs=[pl.BlockSpec(memory_space=pl.ANY)] * 3
        + [pl.BlockSpec(memory_space=pltpu.VMEM)] * 2
        + [pl.BlockSpec(memory_space=pl.ANY)],
        out_specs=(pl.BlockSpec(memory_space=pltpu.VMEM),) * 2
        + (pl.BlockSpec(memory_space=pl.ANY),),
        scratch_shapes=[
            pltpu.VMEM((2 * KEYS, HD), bf16),
            pltpu.VMEM((Q, HD), bf16),
            pltpu.VMEM((2 * KEYS, HD), f32),
            pltpu.VMEM((NX, Q, HD), bf16),
            pltpu.VMEM((NS, KEYS, HD), bf16),
            pltpu.VMEM((NS, HD, KEYS), bf16),
            pltpu.VMEM((NX, HD, Q), f32),
            pltpu.VMEM((NX, 8, Q), f32),
            pltpu.VMEM((NX, 8, Q), f32),
            pltpu.VMEM((2, KEYS, Q), f32),
            pltpu.VMEM((3, HD, Q), bf16),
            pltpu.VMEM((3, HD, Q), bf16),
            pltpu.VMEM((3, Q // 128, 128), f32),
            pltpu.VMEM((3, Q // 128, 128), f32),
            pltpu.VMEM((128, HD), bf16),
            pltpu.VMEM((NX, 24, 128), f32),
            pltpu.VMEM((NZ, 1024, 256), bf16),
            pltpu.VMEM((2, 2, ROWS, 512), bf16),
            pltpu.VMEM((34, 128, 256), bf16),
            pltpu.VMEM((34, 128, 256), bf16),
            dma((5,)),
        ] + [dma((3,))] * 12 + [
            dma((2,)), dma((2,)), dma((4,)), dma((4,)), dma((2,)), dma((2,)),
            dma((NZ,)), dma((NZ,)), dma((3,)), dma((3,)), dma((34,)), dma((34,)),
            dma, dma, dma((6,)), dma((6,)), dma((NZ,)), dma((NZ,)), dma((2,)), dma((2,)),
        ],
        compiler_params=pltpu.CompilerParams(
            collective_id=0, has_side_effects=True, vmem_limit_bytes=60 * 2 ** 20
        ),
        cost_estimate=pl.CostEstimate(
            flops=4 * NX * Q * NS * KEYS * HD, bytes_accessed=4 * 2 ** 20,
            transcendentals=NX * Q * NS * KEYS,
        ),
        name="attention_and_projection",
    )(q, fresh, prefix, probe, pair, w)


def placement_kernel(
    ids_ref, member_ref, rows_hbm, y_ref, dec_ref, out_ref, y_out, dec_out, sem
):
    me = lax.axis_index("inst")
    size = BLK * 2

    def block(b, n):
        return pltpu.make_async_copy(
            rows_hbm.at[pl.ds(b * size, size)], out_ref.at[pl.ds(n * size, size)], sem.at[n]
        )

    def take(b, taken):
        mine = ids_ref[member_ref[b]] == me

        @pl.when(mine)
        def _():
            block(b, taken).start()

        return taken + mine.astype(jnp.int32)

    taken = lax.fori_loop(0, 32, take, 0)

    def clear(n, carry):
        out_ref[pl.ds(n * size, size), :] = jnp.zeros((size, HD), out_ref.dtype)
        return carry

    lax.fori_loop(taken, CAP, clear, 0)
    y_out[...] = y_ref[...]
    dec_out[...] = dec_ref[...]

    def finish(n, carry):
        block(0, n).wait()
        return carry

    lax.fori_loop(0, taken, finish, 0)


def placement(ids, members, rows, y, dec):
    vmem = pl.BlockSpec(memory_space=pltpu.VMEM)
    return pl.pallas_call(
        placement_kernel,
        out_shape=(
            jax.ShapeDtypeStruct((CAP * BLK * 2, HD), jnp.bfloat16),
            jax.ShapeDtypeStruct(y.shape, y.dtype),
            jax.ShapeDtypeStruct(dec.shape, dec.dtype),
        ),
        in_specs=[pl.BlockSpec(memory_space=pltpu.SMEM)] * 2
        + [pl.BlockSpec(memory_space=pl.ANY), vmem, vmem],
        out_specs=(vmem,) * 3,
        scratch_shapes=[pltpu.SemaphoreType.DMA((CAP,))],
        compiler_params=pltpu.CompilerParams(vmem_limit_bytes=60 * 2 ** 20),
        name="placement",
    )(ids, members, rows, y, dec)


def on_device(
    fresh_segment_probes,
    fresh_segment_pairs,
    earlier_stored_pairs,
    emitted_token_probe,
    emitted_token_pair,
    final_projection_weights,
    remaining_instance_ids,
    segment_destination_member,
):
    span_hidden, decode_attention, moved = fused(
        fresh_segment_probes.reshape(Q, HD),
        fresh_segment_pairs.reshape(ROWS * 2, HD),
        earlier_stored_pairs.reshape(4 * ROWS * 2, HD),
        emitted_token_probe,
        emitted_token_pair.reshape(2, HD),
        final_projection_weights,
    )
    cache, span_hidden, decode_attention = placement(
        remaining_instance_ids, segment_destination_member.reshape(-1),
        moved.reshape(-1, HD), span_hidden, decode_attention,
    )
    return span_hidden, cache.reshape(1, CAP * BLK, 2, 1, HD), decode_attention


def solution(mesh):
    return jax.shard_map(
        on_device,
        mesh=mesh,
        in_specs=(
            P("inst", "tp", None),
            P("inst", None, "tp", None),
            P("inst", None, "tp", None),
            P("tp", None),
            P(None, "tp", None),
            P("tp", "inst"),
            P(),
            P(),
        ),
        out_specs=(P("inst", "tp"), P("inst", None, None, "tp", None), P("tp", None)),
        check_vma=False,
    )
```
